256 devices in a mesh: dp: 4 (over x), seq: 64 (over y, z, core).
Axes of the slice: x: 4, y: 4, z: 8, core: 2. Of those that a mesh axis runs over, the one named last changes fastest.
Arguments:
- queries: bfloat16 [4, 8192, 4096], P('dp', 'seq'), may hold values from -120 to 120
- encoded: bfloat16 [4, 64, 12, 128, 896], P('dp', 'seq'), may hold values from -8 to 8
- projection: bfloat16 [896, 8192], P(None, ('dp', 'seq')), may hold values from -0.1875 to 0.1875
- neighbour_shard: int32 [4, 128, 2], P('dp', 'seq'), may hold values from 0 to 3, all different within a row; in each aligned block of 2 rows (0 to 1, 2 to 3, ..., all dimensions but the last counted through in order) at most 2 rows name the same one
- neighbour_block: int32 [4, 128, 2], P('dp', 'seq'), may hold values from 0 to 11
Outputs:
- attended: bfloat16 [4, 8192, 4096], P('dp', 'seq')
The draws below stay inside these ranges and needn't reach their ends.
Inputs may be any that keep to these rules, and one draw needn't show every extreme that they name: `neighbour_shard`: each span's 2 neighbours lie in different shards; among the 2 spans of one device no shard is named more than 2 times, and some device names one shard 2 times.
All inputs are finite; a program needn't handle non-finite values.
Results may differ from the reference program's by a relative error of at most 0.0062.
Values may be sent and summed in bfloat16 or wider, within the bound.
A program may use at most 128 MiB of HBM per device.

```python
import math
import jax
import jax.numpy as jnp
import numpy as np
from jax import lax

D = 4096
HEADS = 32
HD = 128
DE = 896
CH = 64
NL = 128
NBR = 2
CPD = 2
LEN = 8192
NCH = 128
SEQS = 4
BPD = 12
CAP = 2
N_DP = 4
N_SEQ = 64


def draw_queries(key, part):
    values = jax.random.normal(key, (SEQS, LEN, D), jnp.float32)
    return jnp.clip(values, -6.0, 6.0).astype(jnp.bfloat16)


def draw_encoded(key, part):
    values = jax.random.normal(key, (SEQS, N_SEQ, BPD, NL, DE), jnp.float32)
    return jnp.clip(values, -6.0, 6.0).astype(jnp.bfloat16)


def place_ends(drawn, stream_key, low, top_value):
    place = [jax.random.randint(jax.random.fold_in(stream_key, axis), (), 0, length) for axis, length in enumerate(drawn.shape)]
    widest = drawn.shape.index(max(drawn.shape))
    beside = place[:widest] + [(place[widest] + 1) % drawn.shape[widest]] + place[widest + 1:]
    return drawn.at[tuple(place)].set(low).at[tuple(beside)].set(top_value)


def shard_levels(stream_key, dims, cuts, low, largest):
    loudness = 1.0
    for dim, blocks in cuts:
        steps = jax.random.uniform(jax.random.fold_in(jax.random.fold_in(stream_key, 6), dim), (blocks,), jnp.float32, low / len(cuts), largest / len(cuts))
        loudness = loudness * jnp.repeat(jnp.exp(steps), dims[dim] // blocks).reshape((-1,) + (1,) * (len(dims) - 1 - dim))
    return loudness


def assign_block(key, own, number, rows, number_of, top, limit, skew):
    order = jax.random.permutation(key, number_of)
    packed, usual = shares(number_of, rows * top, limit, skew, True), shares(number_of, rows * top, limit, skew, False)
    places = jnp.arange(number_of)

    def named(sizes, offset_by):
        used = int((sizes > 0).sum())
        fixed = max(1, used // 4)
        passed = fixed + (places - fixed + offset_by * (used - fixed)) % max(1, number_of - fixed)
        return jnp.zeros((number_of,), jnp.int32).at[order[jnp.where(places < fixed, places, passed)]].set(jnp.asarray(sizes, jnp.int32))

    sizes = jnp.where(number % 4 == 0, named(packed, number // 4), named(usual, number - number // 4 - 1))
    mixed = jax.random.permutation(jax.random.fold_in(own, 3), number_of)
    donor, receiver = mixed[0:number_of // 2 * 2:2], mixed[1:number_of // 2 * 2:2]
    slack = jnp.minimum(sizes[donor] - 1, limit - sizes[receiver]) // 2
    slack = jnp.where((donor == order[0]) | (receiver == order[0]) | (sizes[receiver] == 0), 0, jnp.maximum(slack, 0))
    passed = jax.random.randint(jax.random.fold_in(own, 4), (number_of // 2,), 0, 1 << 20) % (slack + 1)
    sizes = sizes.at[donor].add(-passed).at[receiver].add(passed)
    labels = jnp.searchsorted(jnp.cumsum(sizes), jnp.arange(rows * top), side="right").astype(jnp.int32)
    listing = labels.reshape(top, rows).T
    listing = listing[jax.random.permutation(jax.random.fold_in(own, 1), rows)]
    offset_by = jax.random.randint(jax.random.fold_in(own, 2), (rows, 1), 0, top)
    return jnp.take_along_axis(listing, (jnp.arange(top)[None, :] + offset_by) % top, axis=1)


def shares(count, total, bound, lean, full):
    loads = [(1 << 20) // math.isqrt(rank ** lean) + 1 for rank in range(1, count + 1)]
    largest = bound if full else min(bound, max(-(-total // count), total * loads[0] // sum(loads)))
    least = 1 if total - largest >= count - 1 else 0
    holding, surplus = [largest] + [least] * (count - 1), total - largest - least * (count - 1)
    while surplus > 0:
        movable = [i for i in range(1, count) if holding[i] < largest] or [i for i in range(1, count) if holding[i] < bound]
        mass, left = sum([loads[i] for i in movable]), surplus
        for i in movable:
            more = min(bound - holding[i], max(1, left * loads[i] // mass), surplus)
            holding[i] = holding[i] + more
            surplus = surplus - more
    return np.array(holding)


def centred(own_key, extent, deviation, bound, cuts=(), kind=jnp.bfloat16):
    factor_of = shard_levels(own_key, extent, cuts, -0.22, 0.18) if cuts else 1.0
    array = jax.random.normal(own_key, extent, jnp.float32) * deviation * factor_of
    return jnp.minimum(jnp.maximum(array, -bound), bound).astype(kind)


def setup_inputs(seed: int = 0) -> dict:
    seeds = jax.random.split(jax.random.key(seed), 6)
    queries = draw_queries(jax.random.fold_in(seeds[5], 71), 0)
    encoded = draw_encoded(jax.random.fold_in(seeds[5], 71), 0)
    projection = centred(seeds[2], (DE, 2 * D), DE ** -0.5, 0.1875, ((1, 256),))
    neighbour_shard_keys = jax.random.split(jax.random.fold_in(seeds[3], 1), SEQS * NCH // CPD)
    neighbour_shard_turns = jax.random.permutation(jax.random.fold_in(seeds[3], 3), SEQS * NCH // CPD)
    neighbour_shard = jax.vmap(lambda own, number: assign_block(jax.random.fold_in(seeds[3], 2), own, number, CPD, N_DP, NBR, CAP, 2))(neighbour_shard_keys, neighbour_shard_turns).reshape((SEQS, NCH, NBR))
    neighbour_block = place_ends(jax.random.randint(seeds[4], (SEQS, NCH, NBR), 0, BPD), jax.random.fold_in(seeds[4], 1), 0, BPD - 1).astype(jnp.int32)
    return dict(queries=queries, encoded=encoded, projection=projection, neighbour_shard=neighbour_shard, neighbour_block=neighbour_block)


def span_attention(span_rows, tokens, projection):
    key_value = jnp.dot(tokens, projection, preferred_element_type=jnp.float32).astype(jnp.bfloat16)
    head_split = key_value.reshape(tokens.shape[0], HEADS, 2, HD).astype(jnp.float32)
    query_split = span_rows.reshape(CH, HEADS, HD).astype(jnp.float32)
    scores = jnp.einsum('ihd,jhd->hij', query_split, head_split[:, :, 0]) * (1.0 / math.sqrt(HD))
    weights = lax.optimization_barrier(jax.nn.softmax(scores, axis=-1).astype(jnp.bfloat16)).astype(jnp.float32)
    combined = jnp.einsum('hij,jhd->ihd', weights, head_split[:, :, 1])
    return combined.astype(jnp.bfloat16).reshape(CH, HEADS * HD)

def reference(queries, encoded, projection, neighbour_shard, neighbour_block):
    shifted = jnp.concatenate([queries[:, CH - 1:], jnp.zeros((SEQS, CH - 1, D), queries.dtype)], axis=1)
    all_span_rows = shifted.reshape(SEQS * NCH, CH, D)
    holder_pos = (jnp.arange(NCH, dtype=jnp.int32) // CPD)[None, :, None]
    flat_index = ((neighbour_shard * N_SEQ + holder_pos) * BPD + neighbour_block).astype(jnp.int32)
    flat_index = flat_index.reshape(SEQS * NCH, NBR)
    all_blocks = encoded.reshape(SEQS * N_SEQ * BPD, NL, DE)

    def one_span(element):
        span_rows, span_picks = element
        tokens = jnp.take(all_blocks, span_picks, axis=0).reshape(NBR * NL, DE)
        return span_attention(span_rows, tokens, projection)
    combined = lax.map(one_span, (all_span_rows, flat_index)).reshape(SEQS, LEN, D)
    leading = jnp.zeros((SEQS, CH - 1, D), combined.dtype)
    return jnp.concatenate([leading, combined[:, :LEN - (CH - 1)]], axis=1)
```

```python
import math

import jax
import jax.numpy as jnp
from jax import lax
from jax.experimental import pallas as pl
from jax.experimental.pallas import tpu as pltpu
from jax.sharding import PartitionSpec as P

MESH = pl.DeviceIdType.MESH
HD = 128
CH = 64
LA = 384
LB = 512
SCALE = 1.0 / math.sqrt(HD)


def dot_nt(a, b):
    return lax.dot_general(a, b, (((1,), (1,)), ((), ())), preferred_element_type=jnp.float32)


def dot_nn(a, b):
    return lax.dot_general(a, b, (((1,), (0,)), ((), ())), preferred_element_type=jnp.float32)


def kernel(
    q_ref, enc_hbm, wt_ref, sh_ref, bl_ref, out_ref,
    WA, WB, enc, packA, packB, recvA, recvB, tokA, tokB, q_all, qs, stage, fix, idx_out, idx_in, idx_smem,
    lsem, ssem, qsem, osem, s_idx, s_tok, s_sib, s_p1x, s_p2z, s_p1y, s_p1z, s_p2x, s_p2y, s_q, s_o,
):
    x = lax.axis_index("dp")
    s = lax.axis_index("seq")
    y = lax.div(s, 16)
    z = lax.rem(lax.div(s, 2), 8)
    k = lax.rem(s, 2)
    yy = lax.div(y, 2)
    cs = lax.rem(y, 2)
    act = cs == k

    def dev(dx=0, dy=0, dz=0, core=None):
        core = k if core is None else core
        return (
            lax.rem(x + dx + 4, 4),
            lax.rem(y + dy + 4, 4) * 16 + lax.rem(z + dz + 8, 8) * 2 + core,
        )

    def chip_along(step, core):
        return (x, lax.rem(lax.div(s, 2) + step + 32, 32) * 2 + core)

    sib = dev(core=1 - k)
    counter = [0]

    def remote(src, dst, rsem, to):
        n = counter[0]
        counter[0] += 1

        def build():
            return pltpu.make_async_remote_copy(
                src_ref=src, dst_ref=dst, send_sem=ssem.at[n], recv_sem=rsem, device_id=to, device_id_type=MESH
            )

        return build

    def arrived(dst, rsem):
        pltpu.make_async_copy(dst, dst, rsem).wait()

    enc_cp = pltpu.make_async_copy(enc_hbm, enc, lsem.at[0])
    enc_cp.start()

    barrier = pltpu.get_barrier_semaphore()
    partners = [sib]
    for c in (0, 1):
        partners += [dev(dx=d, core=c) for d in (1, 2, 3)]
        partners += [dev(dz=d, core=c) for d in range(1, 8)]
        partners += [chip_along(1, c), chip_along(-1, c)]
    partners += [dev(dy=d) for d in (1, 2, 3)]
    for p in partners:
        pl.semaphore_signal(barrier, inc=1, device_id=p, device_id_type=MESH)

    lane = lax.broadcasted_iota(jnp.int32, (8, 128), 1)
    own_sh = [sh_ref[0, e // 2, e % 2] for e in range(4)]
    own_bl = [bl_ref[0, e // 2, e % 2] for e in range(4)]
    codes = jnp.zeros((8, 128), jnp.int32)
    for e in range(4):
        codes = jnp.where(lane == e, own_sh[e], codes)
        codes = jnp.where(lane == 4 + e, own_bl[e], codes)
    idx_out[...] = codes
    pl.semaphore_wait(barrier, len(partners))

    always, if_act, if_pas = [], [], []

    for d in (1, 2, 3):
        always.append(remote(idx_out, idx_in.at[x], s_idx.at[d], dev(dx=d)))
        always[-1]().start()

    wa = wt_ref.at[:, pl.ds(0, LA)]
    wb = wt_ref.at[:, pl.ds(LA, LB)]
    half = pl.ds(pl.multiple_of(k * 32, 32), 32)
    other = pl.ds(pl.multiple_of((1 - k) * 32, 32), 32)
    ownA = lambda: pltpu.make_async_copy(wa, WA.at[x, yy, z, half], lsem.at[1])
    ownB = lambda: pltpu.make_async_copy(wb, WB.at[x, yy, z, half], lsem.at[2])
    sibA = remote(wa, WA.at[x, yy, z, half], s_p1x.at[0, k], sib)
    sibB = remote(wb, WB.at[x, yy, z, half], s_p2z.at[0, k], sib)
    if_pas += [sibA, sibB]

    @pl.when(act)
    def _():
        ownA().start()
        ownB().start()

    @pl.when(jnp.logical_not(act))
    def _():
        sibA().start()
        sibB().start()

    for d in (4, 3, 5, 2, 6, 1, 7):
        always.append(remote(wb, WB.at[x, yy, z, half], s_p2z.at[d, k], dev(dz=d, core=cs)))
        always[-1]().start()
    for d in (2, 1, 3):
        always.append(remote(wa, WA.at[x, yy, z, half], s_p1x.at[d, k], dev(dx=d, core=cs)))
        always[-1]().start()

    enc_cp.wait()
    for d in (1, 2, 3):
        src = lax.rem(x + d, 4)
        arrived(idx_in.at[src], s_idx.at[4 - d])
        cp = pltpu.make_async_copy(idx_in.at[src], idx_smem.at[src], lsem.at[3])
        cp.start()
        cp.wait()

    def wanted(sh, bl):
        m = [v == x for v in sh]
        first = jnp.where(m[0], bl[0], jnp.where(m[1], bl[1], jnp.where(m[2], bl[2], bl[3])))
        last = jnp.where(m[3], bl[3], jnp.where(m[2], bl[2], jnp.where(m[1], bl[1], bl[0])))
        return first, last

    tokB_sends = []
    for d in (2, 1, 3):
        src = lax.rem(x + d, 4)
        pair = wanted([idx_smem[src, 0, e] for e in range(4)], [idx_smem[src, 0, 4 + e] for e in range(4)])
        for i in range(2):
            block = enc[pair[i]]
            packA[d - 1, i] = block[:, :LA]
            packB[d - 1, i] = block[:, LA:]
        mine = pl.ds(x * 2, 2)
        always.append(remote(packA.at[d - 1], recvA.at[mine], s_tok.at[0, d], dev(dx=d)))
        always[-1]().start()
        tokB_sends.append(remote(packB.at[d - 1], recvB.at[mine], s_tok.at[1, d], dev(dx=d)))
    for t in tokB_sends:
        always.append(t)
        t().start()
    pair = wanted(own_sh, own_bl)
    for i in range(2):
        block = enc[pair[i]]
        recvA[x * 2 + i] = block[:, :LA]
        recvB[x * 2 + i] = block[:, LA:]

    p1y = [remote(WA.at[:, yy, z], WA.at[:, yy, z], s_p1y.at[yy], dev(dy=d)) for d in (1, 3, 2)]
    if_act += p1y

    def zstep(direction, step, part):
        plane = lax.rem(z + (8 - (step - 1) if direction == 0 else step - 1), 8)
        return remote(
            WA.at[:, part, plane], WA.at[:, part, plane], s_p1z.at[direction, step - 1, part],
            dev(dz=1 if direction == 0 else -1),
        )

    def zwait(direction, step, part):
        plane = lax.rem(z + (8 - step if direction == 0 else step), 8)
        arrived(WA.at[:, part, plane], s_p1z.at[direction, step - 1, part])

    z_own = [zstep(i, 1, yy) for i in (0, 1)]
    z_far = [zstep(i, 1, 1 - yy) for i in (0, 1)]
    always += z_own + z_far

    p2x = {d: remote(WB.at[x, yy], WB.at[x, yy], s_p2x.at[d], dev(dx=d)) for d in (1, 3, 2)}
    if_act += list(p2x.values())

    def ysend(direction, d, zh, part):
        ref = WB.at[lax.rem(x + d, 4), part, pl.ds(4 * zh, 4)]
        return remote(ref, ref, s_p2y.at[direction, d, zh], dev(dy=1 if direction == 0 else -1))

    def ywait(direction, d, zh):
        part = lax.div(lax.rem(y + (3 if direction == 0 else 1), 4), 2)
        part = jnp.where(act, 1 - yy, part)
        arrived(WB.at[lax.rem(x + d, 4), part, pl.ds(4 * zh, 4)], s_p2y.at[direction, d, zh])

    y_act = {d: [ysend(0, d, 0, yy), ysend(1, d, 1, yy), ysend(0, d, 1, yy), ysend(1, d, 0, yy)] for d in range(4)}
    below, above = lax.div(lax.rem(y + 3, 4), 2), lax.div(lax.rem(y + 1, 4), 2)
    y_pas = {d: [ysend(0, d, 0, below), ysend(1, d, 1, above)] for d in range(4)}
    for d in range(4):
        if_act += y_act[d]
        if_pas += y_pas[d]

    @pl.when(act)
    def _():
        ownA().wait()
        arrived(WA.at[x, yy, z, other], s_p1x.at[0, 1 - k])
        for d in (1, 2, 3):
            for c in (0, 1):
                arrived(WA.at[lax.rem(x + 4 - d, 4), yy, z, pl.ds(c * 32, 32)], s_p1x.at[d, c])
        for t in p1y + z_own:
            t().start()
        ownB().wait()
        arrived(WB.at[x, yy, z, other], s_p2z.at[0, 1 - k])
        for d in range(1, 8):
            for c in (0, 1):
                arrived(WB.at[x, yy, lax.rem(z + 8 - d, 8), pl.ds(c * 32, 32)], s_p2z.at[d, c])
        for t in [p2x[1], p2x[3]] + y_act[0]:
            t().start()
        arrived(WA.at[:, 1 - yy, z], s_p1y.at[1 - yy])
        for t in z_far:
            t().start()

    @pl.when(jnp.logical_not(act))
    def _():
        for part in (0, 1):
            arrived(WA.at[:, part, z], s_p1y.at[part])
        for t in z_own + z_far:
            t().start()

    local_rows = pl.ds(pl.multiple_of(k * 128, 128), 128)

    def qcols(g, core):
        return pl.ds(pl.multiple_of(g * 512 + core * 256, 256), 256)

    def gcols(g):
        return pl.ds(pl.multiple_of(g * 256, 256), 256)

    def q_copies(g):
        loc = pltpu.make_async_copy(q_ref.at[:, qcols(g, k)], q_all.at[local_rows, gcols(g)], lsem.at[4])
        to_sib = pltpu.make_async_remote_copy(
            src_ref=q_ref.at[:, qcols(g, 1 - k)], dst_ref=q_all.at[local_rows, gcols(g)],
            send_sem=qsem.at[0], recv_sem=s_q.at[0], device_id=sib, device_id_type=MESH,
        )
        back = [
            pltpu.make_async_remote_copy(
                src_ref=q_ref.at[pl.ds(0, 64), qcols(g, c)], dst_ref=q_all.at[pl.ds(256, 64), gcols(g)],
                send_sem=qsem.at[1 + c], recv_sem=s_q.at[1], device_id=chip_along(-1, c), device_id_type=MESH,
            )
            for c in (0, 1)
        ]
        return loc, to_sib, back

    @pl.loop(0, 8)
    def _(g):
        loc, to_sib, back = q_copies(g)
        loc.start()
        to_sib.start()

        @pl.when(k == 0)
        def _():
            back[0].start()
            back[1].start()

    z_next = {st: [zstep(i, st, p) for i in (0, 1) for p in (0, 1)] for st in (2, 3)}
    z_last = [zstep(0, 4, 0), zstep(1, 4, 1)]
    for st in (2, 3):
        always += z_next[st]
    always += z_last

    def z_forward(st):
        n = 0
        for i in (0, 1):
            for p in (0, 1):
                zwait(i, st - 1, p)
                if st < 4:
                    z_next[st][n]().start()
                elif i == p:
                    z_last[i]().start()
                n += 1

    def y_forward(d):
        for first in (0, 1):
            ywait(0, d, first)
            ywait(1, d, 1 - first)
            if first == 0:
                y_pas[d][0]().start()
                y_pas[d][1]().start()

    @pl.when(jnp.logical_not(act))
    def _():
        y_forward(0)

    z_forward(2)

    @pl.when(act)
    def _():
        for d in (1, 3):
            arrived(WB.at[lax.rem(x + 4 - d, 4), yy], s_p2x.at[d])
            for t in y_act[4 - d]:
                t().start()
        p2x[2]().start()

    @pl.when(jnp.logical_not(act))
    def _():
        y_forward(3)

    z_forward(3)

    half_tok = []
    rank = [jnp.int32(0)]
    for e in range(1, 4):
        same = own_sh[e] == own_sh[0]
        for f in range(1, e):
            same = jnp.logical_or(same, own_sh[e] == own_sh[f])
        rank.append(jnp.where(same, 1, 0))
    for which, (recv, tok) in enumerate(((recvA, tokA), (recvB, tokB))):
        for d in (1, 2, 3):
            arrived(recv.at[pl.ds(lax.rem(x + 4 - d, 4) * 2, 2)], s_tok.at[which, d])
        for e in range(4):
            tok[k, pl.ds(e * 128, 128)] = recv[own_sh[e] * 2 + rank[e]]
        half_tok.append(remote(tok.at[k], tok.at[k], s_sib.at[which], sib))
        half_tok[-1]().start()
    always += half_tok

    @pl.when(act)
    def _():
        arrived(WB.at[lax.rem(x + 2, 4), yy], s_p2x.at[2])
        for t in y_act[2]:
            t().start()

    @pl.when(jnp.logical_not(act))
    def _():
        y_forward(1)
        y_forward(2)

    z_forward(4)

    whole_q = q_all.at[pl.ds(0, 128)]
    pltpu.make_async_copy(q_ref.at[:, pl.ds(0, 2048)], whole_q, lsem.at[4]).wait()
    arrived(whole_q, s_q.at[0])
    arrived(q_all.at[pl.ds(256, 64)], s_q.at[1])

    @pl.loop(0, 8)
    def _(g):
        rows = q_all[pl.ds(48, 272), gcols(g)].astype(jnp.float32)
        qs[:, gcols(g)] = pltpu.roll(rows, 1, 0)[16:].astype(jnp.bfloat16)

    for which, tok in enumerate((tokA, tokB)):
        arrived(tok.at[1 - k], s_sib.at[which])
    zwait(0, 4, 0)
    zwait(1, 4, 1)

    @pl.when(act)
    def _():
        for d in range(4):
            ywait(0, d, 0)
            ywait(1, d, 1)

    def out_copies(g):
        cols = qcols(g, k)
        mids = pl.ds(pl.multiple_of((1 - k) * 64, 64), 128)
        to_next = pltpu.make_async_remote_copy(
            src_ref=stage.at[g, pl.ds(192, 64)], dst_ref=out_ref.at[pl.ds(0, 64), cols],
            send_sem=osem.at[0], recv_sem=s_o.at[k], device_id=chip_along(1, 0), device_id_type=MESH,
        )
        del mids
        zero = pltpu.make_async_remote_copy(
            src_ref=stage.at[g, pl.ds(64, 128)], dst_ref=out_ref.at[:, cols],
            send_sem=osem.at[1], recv_sem=s_o.at[2], device_id=sib, device_id_type=MESH,
        )
        one = pltpu.make_async_remote_copy(
            src_ref=stage.at[g, pl.ds(0, 64)], dst_ref=out_ref.at[pl.ds(64, 64), cols],
            send_sem=osem.at[2], recv_sem=s_o.at[3], device_id=sib, device_id_type=MESH,
        )
        edge = pltpu.make_async_remote_copy(
            src_ref=stage.at[g, pl.ds(240, 16)], dst_ref=fix.at[:, cols],
            send_sem=osem.at[3], recv_sem=s_o.at[4], device_id=sib, device_id_type=MESH,
        )
        return to_next, zero, one, edge

    @pl.loop(0, 8)
    def _(g):
        xg, yg = lax.div(g, 2), lax.rem(g, 2)
        for zh in (0, 1):
            wa_h = WA[xg, yg, pl.ds(4 * zh, 4)].reshape(256, LA)
            wb_h = WB[xg, yg, pl.ds(4 * zh, 4)].reshape(256, LB)
            cols = pl.ds(pl.multiple_of(g * 256 + zh * 128, 128), 128)
            parts = []
            for j in range(4):
                rows = pl.ds((j % 2) * 256, 256)
                kv = dot_nt(wa_h, tokA[j // 2, rows]) + dot_nt(wb_h, tokB[j // 2, rows])
                kv = kv.astype(jnp.bfloat16)
                sc = dot_nn(qs[pl.ds(j * 64, 64), cols], kv[:128]) * SCALE
                sc = jnp.exp(sc - jnp.max(sc, axis=1, keepdims=True))
                w = (sc / jnp.sum(sc, axis=1, keepdims=True)).astype(jnp.bfloat16)
                parts.append(dot_nt(w, kv[128:]))
            comb = pltpu.roll(jnp.concatenate(parts, axis=0), 255, 0)
            stage[g, :, pl.ds(zh * 128, 128)] = comb.astype(jnp.bfloat16)
        to_next, zero, one, edge = out_copies(g)
        to_next.start()

        @pl.when(k == 0)
        def _():
            zero.start()
            out_ref[pl.ds(64, 64), qcols(g, 0)] = stage[g, pl.ds(0, 64)]
            fix[:, qcols(g, 0)] = stage[g, pl.ds(240, 16)]

        @pl.when(k == 1)
        def _():
            one.start()
            edge.start()
            out_ref[:, qcols(g, 1)] = stage[g, pl.ds(64, 128)]

    pltpu.make_async_copy(q_all.at[pl.ds(0, 64)], q_all.at[pl.ds(0, 64)], osem.at[0]).wait()
    pltpu.make_async_copy(whole_q, whole_q, qsem.at[0]).wait()

    @pl.when(k == 0)
    def _():
        sixty_four = q_all.at[pl.ds(0, 64)]
        sixteen = q_all.at[pl.ds(0, 16)]
        arrived(sixty_four, qsem.at[1])
        arrived(sixty_four, qsem.at[2])
        arrived(whole_q, osem.at[1])
        arrived(sixty_four, s_o.at[0])
        arrived(sixty_four, s_o.at[1])
        arrived(sixty_four, s_o.at[3])
        arrived(sixteen, s_o.at[4])
        first = s == 0

        @pl.when(first)
        def _():
            out_ref[pl.ds(0, 48)] = jnp.zeros((48, 4096), jnp.bfloat16)

        @pl.loop(0, 8)
        def _(g):
            cols = pl.ds(pl.multiple_of(g * 512, 512), 512)
            row = lax.broadcasted_iota(jnp.int32, (16, 512), 0)
            came = out_ref[pl.ds(48, 16), cols].astype(jnp.float32)
            came = jnp.where(first, 0.0, came)
            own = fix[:, cols].astype(jnp.float32)
            out_ref[pl.ds(48, 16), cols] = jnp.where(row == 15, own, came).astype(jnp.bfloat16)

    @pl.when(k == 1)
    def _():
        arrived(q_all.at[pl.ds(0, 64)], osem.at[2])
        arrived(q_all.at[pl.ds(0, 16)], osem.at[3])
        arrived(whole_q, s_o.at[2])

    for t in always:
        t().wait_send()

    @pl.when(act)
    def _():
        for t in if_act:
            t().wait_send()

    @pl.when(jnp.logical_not(act))
    def _():
        for t in if_pas:
            t().wait_send()


def body(queries, encoded, projection, neighbour_shard, neighbour_block):
    bf = jnp.bfloat16
    dma = pltpu.SemaphoreType.DMA
    hbm = pl.BlockSpec(memory_space=pl.ANY)
    smem = pl.BlockSpec(memory_space=pltpu.SMEM)
    out = pl.pallas_call(
        kernel,
        name="spans",
        out_shape=jax.ShapeDtypeStruct((128, 4096), bf),
        in_specs=[hbm, hbm, hbm, smem, smem],
        out_specs=pl.BlockSpec(memory_space=pltpu.VMEM),
        scratch_shapes=[
            pltpu.VMEM((4, 2, 8, 64, LA), bf),
            pltpu.VMEM((4, 2, 8, 64, LB), bf),
            pltpu.VMEM((12, 128, 896), bf),
            pltpu.VMEM((3, 2, 128, LA), bf),
            pltpu.VMEM((3, 2, 128, LB), bf),
            pltpu.VMEM((8, 128, LA), bf),
            pltpu.VMEM((8, 128, LB), bf),
            pltpu.VMEM((2, 512, LA), bf),
            pltpu.VMEM((2, 512, LB), bf),
            pltpu.VMEM((320, 2048), bf),
            pltpu.VMEM((256, 2048), bf),
            pltpu.VMEM((8, 256, 256), bf),
            pltpu.VMEM((16, 4096), bf),
            pltpu.VMEM((8, 128), jnp.int32),
            pltpu.VMEM((4, 8, 128), jnp.int32),
            pltpu.SMEM((4, 8, 128), jnp.int32),
            dma((5,)),
            dma((80,)),
            dma((3,)),
            dma((4,)),
            dma((4,)),
            dma((2, 4)),
            dma((2,)),
            dma((4, 2)),
            dma((8, 2)),
            dma((2,)),
            dma((2, 4, 2)),
            dma((4,)),
            dma((2, 4, 2)),
            dma((2,)),
            dma((5,)),
        ],
        compiler_params=pltpu.CompilerParams(
            collective_id=0, has_side_effects=True, vmem_limit_bytes=48 * 2**20
        ),
        cost_estimate=pl.CostEstimate(flops=8 * 10**9, bytes_accessed=6 * 2**20, transcendentals=10**6),
    )(queries[0], encoded[0, 0], projection.T, neighbour_shard, neighbour_block)
    return out[None]


def solution(mesh):
    placed = (
        P("dp", "seq", None),
        P("dp", "seq", None, None, None),
        P(None, ("dp", "seq")),
        P("dp", "seq", None),
        P("dp", "seq", None),
    )
    return jax.shard_map(
        body, mesh=mesh, in_specs=placed, out_specs=P("dp", "seq", None), check_vma=False
    )
```

```python
import math

import jax
import jax.numpy as jnp
from jax import lax
from jax.experimental import pallas as pl
from jax.experimental.pallas import tpu as pltpu
from jax.sharding import PartitionSpec as P

MESH = pl.DeviceIdType.MESH
HD = 128
CH = 64
LA = 384
LB = 512
SCALE = 1.0 / math.sqrt(HD)


def dot_nt(a, b):
    return lax.dot_general(a, b, (((1,), (1,)), ((), ())), preferred_element_type=jnp.float32)


def dot_nn(a, b):
    return lax.dot_general(a, b, (((1,), (0,)), ((), ())), preferred_element_type=jnp.float32)


XS = {0: 0, 3: 1, 1: 2, 2: 3}
XR = (0, 3, 1, 2)
ZS = {0: 0, 1: 1, 7: 2, 2: 3, 6: 4, 3: 5, 5: 6, 4: 7}
DO_P1 = DO_P2 = DO_TOK = DO_Q = DO_OUT = DO_MATH = True


def kernel(
    q_ref, enc_hbm, wt_ref, sh_hbm, bl_hbm, out_ref,
    WA, WB, KV, enc, packA, packB, recvA, recvB, tokA, tokB, q_all, qs, stage, fix, idx_out, idx_in, idx_smem,
    sh_ref, bl_ref,
    lsem, ssem, qsem, osem, s_idx, s_tok, s_sib, s_p1x, s_p2z, s_p1y, s_p1z, s_p2x, s_p2y, s_q, s_o,
):
    x = lax.axis_index("dp")
    s = lax.axis_index("seq")
    y = lax.div(s, 16)
    z = lax.rem(lax.div(s, 2), 8)
    k = lax.rem(s, 2)
    yy = lax.div(y, 2)
    cs = lax.rem(y, 2)
    act = cs == k
    pas = jnp.logical_not(act)

    def dev(dx=0, dy=0, dz=0, core=None):
        core = k if core is None else core
        return (
            lax.rem(x + dx + 4, 4),
            lax.rem(y + dy + 4, 4) * 16 + lax.rem(z + dz + 8, 8) * 2 + core,
        )

    def chip_along(step, core):
        return (x, lax.rem(lax.div(s, 2) + step + 32, 32) * 2 + core)

    sib = dev(core=1 - k)
    counter = [0]

    def remote(src, dst, rsem, to):
        n = counter[0]
        counter[0] += 1

        def build():
            return pltpu.make_async_remote_copy(
                src_ref=src, dst_ref=dst, send_sem=ssem.at[n], recv_sem=rsem, device_id=to, device_id_type=MESH
            )

        return build

    def arrived(dst, rsem):
        pltpu.make_async_copy(dst, dst, rsem).wait()

    sh_cp = pltpu.make_async_copy(sh_hbm, sh_ref, lsem.at[5])
    bl_cp = pltpu.make_async_copy(bl_hbm, bl_ref, lsem.at[6])
    sh_cp.start()
    bl_cp.start()
    enc_cp = pltpu.make_async_copy(enc_hbm, enc, lsem.at[0])
    enc_cp.start()

    barrier = pltpu.get_barrier_semaphore()
    partners = [sib]
    for c in (0, 1):
        partners += [dev(dx=d, core=c) for d in (1, 2, 3)]
        partners += [dev(dz=d, core=c) for d in range(1, 8)]
        partners += [chip_along(1, c), chip_along(-1, c)]
    partners += [dev(dy=d) for d in (1, 2, 3)]
    for p in partners:
        pl.semaphore_signal(barrier, inc=1, device_id=p, device_id_type=MESH)

    lane = lax.broadcasted_iota(jnp.int32, (8, 128), 1)
    sh_cp.wait()
    bl_cp.wait()
    own_sh = [sh_ref[0, e // 2, e % 2] for e in range(4)]
    own_bl = [bl_ref[0, e // 2, e % 2] for e in range(4)]
    codes = jnp.zeros((8, 128), jnp.int32)
    for e in range(4):
        codes = jnp.where(lane == e, own_sh[e], codes)
        codes = jnp.where(lane == 4 + e, own_bl[e], codes)
    idx_out[...] = codes
    pl.semaphore_wait(barrier, len(partners))

    always, if_act, if_pas = [], [], []

    for d in (1, 2, 3):
        always.append(remote(idx_out, idx_in.at[x], s_idx.at[d], dev(dx=d)))
        always[-1]().start()

    wa = wt_ref.at[:, pl.ds(0, LA)]
    wb = wt_ref.at[:, pl.ds(LA, LB)]
    half = pl.ds(pl.multiple_of(k * 32, 32), 32)
    other = pl.ds(pl.multiple_of((1 - k) * 32, 32), 32)
    ownA = lambda: pltpu.make_async_copy(wa, WA.at[0, yy, 0, half], lsem.at[1])
    ownB = lambda: pltpu.make_async_copy(wb, WB.at[0, yy, 0, half], lsem.at[2])
    sibA = remote(wa, WA.at[0, yy, 0, half], s_p1x.at[0, k], sib)
    sibB = remote(wb, WB.at[0, yy, 0, half], s_p2z.at[0, k], sib)
    if_pas += [sibA, sibB]

    @pl.when(act)
    def _():
        ownA().start()
        ownB().start()

    @pl.when(pas)
    def _():
        sibA().start()
        sibB().start()

    for d in (4, 3, 5, 2, 6, 1, 7):
        always.append(remote(wb, WB.at[0, yy, ZS[8 - d], half], s_p2z.at[d, k], dev(dz=d, core=cs)))
        always[-1]().start()
    for d in (2, 1, 3):
        always.append(remote(wa, WA.at[XS[4 - d], yy, 0, half], s_p1x.at[d, k], dev(dx=d, core=cs)))
        always[-1]().start()

    local_rows = pl.ds(pl.multiple_of(k * 128, 128), 128)

    def qcols(g, core):
        return pl.ds(pl.multiple_of(g * 512 + core * 256, 256), 256)

    def gcols(g):
        return pl.ds(pl.multiple_of(g * 256, 256), 256)

    def q_copies(g):
        loc = pltpu.make_async_copy(q_ref.at[:, qcols(g, k)], q_all.at[local_rows, gcols(g)], lsem.at[4])
        to_sib = pltpu.make_async_remote_copy(
            src_ref=q_ref.at[:, qcols(g, 1 - k)], dst_ref=q_all.at[local_rows, gcols(g)],
            send_sem=qsem.at[0], recv_sem=s_q.at[0], device_id=sib, device_id_type=MESH,
        )
        back = [
            pltpu.make_async_remote_copy(
                src_ref=q_ref.at[pl.ds(0, 64), qcols(g, c)], dst_ref=q_all.at[pl.ds(256, 64), gcols(g)],
                send_sem=qsem.at[1 + c], recv_sem=s_q.at[1], device_id=chip_along(-1, c), device_id_type=MESH,
            )
            for c in (0, 1)
        ]
        return loc, to_sib, back

    if DO_Q:
        @pl.loop(0, 8)
        def _(g):
            loc, to_sib, back = q_copies(g)
            loc.start()
            to_sib.start()

            @pl.when(k == 0)
            def _():
                back[0].start()
                back[1].start()

    enc_cp.wait()

    def wanted(sh, bl):
        m = [v == x for v in sh]
        first = jnp.where(m[0], bl[0], jnp.where(m[1], bl[1], jnp.where(m[2], bl[2], bl[3])))
        last = jnp.where(m[3], bl[3], jnp.where(m[2], bl[2], jnp.where(m[1], bl[1], bl[0])))
        return first, last

    to_smem = {}
    for d in (1, 3, 2):
        src = lax.rem(x + d, 4)
        arrived(idx_in.at[src], s_idx.at[4 - d])
        to_smem[d] = pltpu.make_async_copy(idx_in.at[src], idx_smem.at[src], lsem.at[6 + d])
        to_smem[d].start()
    tokB_sends = []
    for d in (1, 3, 2):
        src = lax.rem(x + d, 4)
        to_smem[d].wait()
        pair = wanted([idx_smem[src, 0, e] for e in range(4)], [idx_smem[src, 0, 4 + e] for e in range(4)])
        for i in range(2):
            block = enc[pair[i]]
            packA[d - 1, i] = block[:, :LA]
            packB[d - 1, i] = block[:, LA:]
        mine = pl.ds(x * 2, 2)
        if DO_TOK:
            always.append(remote(packA.at[d - 1], recvA.at[mine], s_tok.at[0, d], dev(dx=d)))
            always[-1]().start()
            tokB_sends.append(remote(packB.at[d - 1], recvB.at[mine], s_tok.at[1, d], dev(dx=d)))
    pair = wanted(own_sh, own_bl)
    for i in range(2):
        block = enc[pair[i]]
        recvA[x * 2 + i] = block[:, :LA]
        recvB[x * 2 + i] = block[:, LA:]

    p1y = [remote(WA.at[:, yy, 0], WA.at[:, yy, 0], s_p1y.at[yy], dev(dy=d)) for d in (1, 3, 2)]
    if_act += p1y

    def zstep(direction, step, part):
        have, there = (step - 1, step) if direction else ((9 - step) % 8, 8 - step)
        return remote(
            WA.at[:, part, ZS[have]], WA.at[:, part, ZS[there]], s_p1z.at[direction, step - 1, part],
            dev(dz=-1 if direction else 1),
        )

    def zwait(direction, step, part):
        arrived(WA.at[:, part, ZS[step if direction else 8 - step]], s_p1z.at[direction, step - 1, part])

    z_own = [zstep(i, 1, yy) for i in (0, 1)]
    z_far = [zstep(i, 1, 1 - yy) for i in (0, 1)]
    z_next = {st: [(i, p, zstep(i, st, p)) for p in (0, 1) for i in (0, 1)] for st in (2, 3)}
    z_next[4] = [(0, 0, zstep(0, 4, 0)), (1, 1, zstep(1, 4, 1))]
    always += z_own + z_far + [t for st in (2, 3, 4) for _, _, t in z_next[st]]

    def z_forward(st):
        if not DO_P1:
            return
        waited = set()
        for i, p, t in z_next[st]:
            zwait(i, st - 1, p)
            waited.add((i, p))
            t().start()
        for i in (0, 1):
            for p in (0, 1):
                if (i, p) not in waited:
                    zwait(i, st - 1, p)

    p2x = {d: remote(WB.at[0, yy], WB.at[XS[4 - d], yy], s_p2x.at[d], dev(dx=d)) for d in (1, 3, 2)}
    if_act += list(p2x.values())

    def ysend(direction, d, piece, part):
        ref = WB.at[XS[d], part, pl.ds(4 * piece, 4)]
        return remote(ref, ref, s_p2y.at[direction, d, piece], dev(dy=-1 if direction else 1))

    below, above = lax.div(lax.rem(y + 3, 4), 2), lax.div(lax.rem(y + 1, 4), 2)

    def ywait(direction, d, piece):
        part = jnp.where(act, 1 - yy, above if direction else below)
        arrived(WB.at[XS[d], part, pl.ds(4 * piece, 4)], s_p2y.at[direction, d, piece])

    y_act = {d: [ysend(0, d, 0, yy), ysend(1, d, 1, yy), ysend(0, d, 1, yy), ysend(1, d, 0, yy)] for d in range(4)}
    y_pas = {d: [ysend(0, d, 0, below), ysend(1, d, 1, above)] for d in range(4)}
    for d in range(4):
        if_act += y_act[d]
        if_pas += y_pas[d]

    def y_forward(d):
        if not DO_P2:
            return
        ywait(0, d, 0)
        y_pas[d][0]().start()
        ywait(1, d, 1)
        y_pas[d][1]().start()
        ywait(0, d, 1)
        ywait(1, d, 0)

    @pl.when(act)
    def _():
        ownA().wait()
        arrived(WA.at[0, yy, 0, other], s_p1x.at[0, 1 - k])
        for d in (1, 2, 3):
            for c in (0, 1):
                arrived(WA.at[XS[4 - d], yy, 0, pl.ds(c * 32, 32)], s_p1x.at[d, c])
        if DO_P1:
            for t in p1y + z_own:
                t().start()
        ownB().wait()
        arrived(WB.at[0, yy, 0, other], s_p2z.at[0, 1 - k])
        for d in range(1, 8):
            for c in (0, 1):
                arrived(WB.at[0, yy, ZS[8 - d], pl.ds(c * 32, 32)], s_p2z.at[d, c])
        if DO_P2:
            for t in [p2x[1], p2x[3]] + y_act[0]:
                t().start()
        if DO_P1:
            arrived(WA.at[:, 1 - yy, 0], s_p1y.at[1 - yy])
            for t in z_far:
                t().start()

    if DO_P1:
        @pl.when(pas)
        def _():
            for part in (0, 1):
                arrived(WA.at[:, part, 0], s_p1y.at[part])
            for t in z_own + z_far:
                t().start()

    if DO_TOK:
        for t in tokB_sends:
            always.append(t)
            t().start()

    whole_q = q_all.at[pl.ds(0, 128)]
    if DO_Q:
        pltpu.make_async_copy(q_ref.at[:, pl.ds(0, 2048)], whole_q, lsem.at[4]).wait()
        arrived(whole_q, s_q.at[0])
        arrived(q_all.at[pl.ds(256, 64)], s_q.at[1])

        @pl.loop(0, 8)
        def _(g):
            rows = q_all[pl.ds(48, 272), gcols(g)].astype(jnp.float32)
            qs[:, gcols(g)] = pltpu.roll(rows, 1, 0)[16:].astype(jnp.bfloat16)

    @pl.when(pas)
    def _():
        y_forward(0)

    z_forward(2)

    if DO_P2:
        @pl.when(act)
        def _():
            for d in (1, 3):
                arrived(WB.at[XS[4 - d], yy], s_p2x.at[d])
                for t in y_act[4 - d]:
                    t().start()
            p2x[2]().start()

    half_tok = []
    rank = [jnp.int32(0)]
    for e in range(1, 4):
        same = own_sh[e] == own_sh[0]
        for f in range(1, e):
            same = jnp.logical_or(same, own_sh[e] == own_sh[f])
        rank.append(jnp.where(same, 1, 0))

    def take_tokens(which):
        recv, tok = ((recvA, tokA), (recvB, tokB))[which]
        if DO_TOK:
            for d in (1, 2, 3):
                arrived(recv.at[pl.ds(lax.rem(x + 4 - d, 4) * 2, 2)], s_tok.at[which, d])
        for e in range(4):
            tok[k, pl.ds(e * 128, 128)] = recv[own_sh[e] * 2 + rank[e]]
        half_tok.append(remote(tok.at[k], tok.at[k], s_sib.at[which], sib))
        half_tok[-1]().start()

    take_tokens(0)

    @pl.when(pas)
    def _():
        y_forward(3)

    z_forward(3)
    take_tokens(1)

    def project(x0, x1, z0, z1):
        if not DO_MATH:
            return
        rows = (x1 - x0) * 2 * (z1 - z0) * 64
        a = WA[x0:x1, :, z0:z1].reshape(rows, LA)
        b = WB[x0:x1, :, z0:z1].reshape(rows, LB)
        for j in range(4):
            at = pl.ds((j % 2) * 256, 256)
            kv = dot_nt(a, tokA[j // 2, at]) + dot_nt(b, tokB[j // 2, at])
            KV[x0:x1, :, z0:z1, :, j * 256 : j * 256 + 256] = kv.astype(jnp.bfloat16).reshape(
                x1 - x0, 2, z1 - z0, 64, 256
            )

    def plane_of(zabs):
        d = lax.rem(zabs - z + 8, 8)
        return jnp.where(d <= 4, jnp.maximum(2 * d - 1, 0), 16 - 2 * d)

    def attend(xs, zh):
        xa = lax.rem(x + XR[xs], 4)
        if not DO_MATH:
            for part in (0, 1):
                stage[xs * 2 + part, :, pl.ds(pl.multiple_of(zh * 128, 128), 128)] = qs[:, 0:128]
            return
        planes = [plane_of(zh * 4 + i) for i in range(4)]
        units = [(part, j) for part in (0, 1) for j in range(4)]
        scores = []
        for part, j in units:
            cols = pl.ds(pl.multiple_of((xa * 2 + part) * 256 + zh * 128, 128), 128)
            at = slice(j * 256, j * 256 + 256)
            keys = jnp.concatenate([KV[xs, part, planes[0], :, at], KV[xs, part, planes[1], :, at]], axis=0)
            scores.append(dot_nn(qs[j * 64 : j * 64 + 64, cols], keys))
        weights = []
        for sc in scores:
            sc = sc * SCALE
            sc = jnp.exp(sc - jnp.max(sc, axis=1, keepdims=True))
            weights.append((sc * (1.0 / jnp.sum(sc, axis=1, keepdims=True))).astype(jnp.bfloat16))
        parts = []
        for (part, j), w in zip(units, weights):
            at = slice(j * 256, j * 256 + 256)
            values = jnp.concatenate([KV[xs, part, planes[2], :, at], KV[xs, part, planes[3], :, at]], axis=0)
            parts.append(dot_nt(w, values))
        for part in (0, 1):
            comb = pltpu.roll(jnp.concatenate(parts[part * 4 : part * 4 + 4], axis=0), 255, 0)
            stage[xs * 2 + part, :, pl.ds(pl.multiple_of(zh * 128, 128), 128)] = comb.astype(jnp.bfloat16)

    def send_out(xs):
        xa = lax.rem(x + XR[xs], 4)
        for part in (0, 1):
            g = xa * 2 + part
            st = stage.at[xs * 2 + part]
            cols = qcols(g, k)

            def to(src, dst, n, target):
                return pltpu.make_async_remote_copy(
                    src_ref=src, dst_ref=dst, send_sem=osem.at[n], recv_sem=s_o.at[n + 1 if n else k],
                    device_id=target, device_id_type=MESH,
                )

            if DO_OUT:
                to(st.at[pl.ds(192, 64)], out_ref.at[pl.ds(0, 64), cols], 0, chip_along(1, 0)).start()

            @pl.when(k == 0)
            def _():
                if DO_OUT:
                    to(st.at[pl.ds(64, 128)], out_ref.at[:, cols], 1, sib).start()
                out_ref[pl.ds(64, 64), qcols(g, 0)] = st[pl.ds(0, 64)]
                fix[:, qcols(g, 0)] = st[pl.ds(240, 16)]

            @pl.when(k == 1)
            def _():
                if DO_OUT:
                    to(st.at[pl.ds(0, 64)], out_ref.at[pl.ds(64, 64), cols], 2, sib).start()
                    to(st.at[pl.ds(240, 16)], fix.at[:, cols], 3, sib).start()
                out_ref[:, qcols(g, 1)] = st[pl.ds(64, 128)]

    near = lax.div(z, 4)
    arrived(tokA.at[1 - k], s_sib.at[0])
    arrived(tokB.at[1 - k], s_sib.at[1])

    def y_here(d):
        if DO_P2:
            ywait(0, d, 0)
            ywait(1, d, 1)

    @pl.when(act)
    def _():
        y_here(0)

    project(0, 1, 0, 5)

    @pl.when(act)
    def _():
        y_here(3)

    project(1, 2, 0, 5)
    z_forward(4)
    project(0, 2, 5, 7)

    @pl.when(act)
    def _():
        if DO_P2:
            arrived(WB.at[XS[2], yy], s_p2x.at[2])
            for t in y_act[2]:
                t().start()
        y_here(1)

    @pl.when(pas)
    def _():
        y_forward(1)

    project(2, 3, 0, 7)
    attend(0, near)
    attend(1, near)
    attend(2, near)

    @pl.when(pas)
    def _():
        y_forward(2)

    if DO_P1:
        zwait(0, 4, 0)
        zwait(1, 4, 1)
    project(0, 3, 7, 8)
    for xs in range(3):
        attend(xs, 1 - near)
        send_out(xs)

    @pl.when(act)
    def _():
        y_here(2)

    project(3, 4, 0, 8)
    attend(3, near)
    attend(3, 1 - near)
    send_out(3)

    always += half_tok
    sixty_four = q_all.at[pl.ds(0, 64)]
    sixteen = q_all.at[pl.ds(0, 16)]
    if DO_Q:
        arrived(whole_q, qsem.at[0])

        @pl.when(k == 0)
        def _():
            arrived(sixty_four, qsem.at[1])
            arrived(sixty_four, qsem.at[2])

    if DO_OUT:
        arrived(sixty_four, osem.at[0])

        @pl.when(k == 0)
        def _():
            arrived(whole_q, osem.at[1])
            arrived(sixty_four, s_o.at[0])
            arrived(sixty_four, s_o.at[1])
            arrived(sixty_four, s_o.at[3])
            arrived(sixteen, s_o.at[4])
            first = s == 0

            @pl.when(first)
            def _():
                out_ref[pl.ds(0, 48)] = jnp.zeros((48, 4096), jnp.bfloat16)

            @pl.loop(0, 8)
            def _(g):
                cols = pl.ds(pl.multiple_of(g * 512, 512), 512)
                row = lax.broadcasted_iota(jnp.int32, (16, 512), 0)
                came = out_ref[pl.ds(48, 16), cols].astype(jnp.float32)
                came = jnp.where(first, 0.0, came)
                own = fix[:, cols].astype(jnp.float32)
                out_ref[pl.ds(48, 16), cols] = jnp.where(row == 15, own, came).astype(jnp.bfloat16)

        @pl.when(k == 1)
        def _():
            arrived(sixty_four, osem.at[2])
            arrived(sixteen, osem.at[3])
            arrived(whole_q, s_o.at[2])

    skip = set()
    if not DO_P1:
        skip |= set(p1y + z_own + z_far + [t for st in (2, 3, 4) for _, _, t in z_next[st]])
    if not DO_P2:
        skip |= set(list(p2x.values()) + [t for d in range(4) for t in y_act[d] + y_pas[d]])
    for t in always:
        if t not in skip:
            t().wait_send()

    @pl.when(act)
    def _():
        for t in if_act:
            if t not in skip:
                t().wait_send()

    @pl.when(pas)
    def _():
        for t in if_pas:
            if t not in skip:
                t().wait_send()


def body(queries, encoded, projection, neighbour_shard, neighbour_block):
    bf = jnp.bfloat16
    dma = pltpu.SemaphoreType.DMA
    hbm = pl.BlockSpec(memory_space=pl.ANY)
    out = pl.pallas_call(
        kernel,
        name="spans",
        out_shape=jax.ShapeDtypeStruct((128, 4096), bf),
        in_specs=[hbm] * 5,
        out_specs=pl.BlockSpec(memory_space=pltpu.VMEM),
        scratch_shapes=[
            pltpu.VMEM((4, 2, 8, 64, LA), bf),
            pltpu.VMEM((4, 2, 8, 64, LB), bf),
            pltpu.VMEM((4, 2, 8, 64, 1024), bf),
            pltpu.VMEM((12, 128, 896), bf),
            pltpu.VMEM((3, 2, 128, LA), bf),
            pltpu.VMEM((3, 2, 128, LB), bf),
            pltpu.VMEM((8, 128, LA), bf),
            pltpu.VMEM((8, 128, LB), bf),
            pltpu.VMEM((2, 512, LA), bf),
            pltpu.VMEM((2, 512, LB), bf),
            pltpu.VMEM((320, 2048), bf),
            pltpu.VMEM((256, 2048), bf),
            pltpu.VMEM((8, 256, 256), bf),
            pltpu.VMEM((16, 4096), bf),
            pltpu.VMEM((8, 128), jnp.int32),
            pltpu.VMEM((4, 8, 128), jnp.int32),
            pltpu.SMEM((4, 8, 128), jnp.int32),
            pltpu.SMEM((1, 2, 2), jnp.int32),
            pltpu.SMEM((1, 2, 2), jnp.int32),
            dma((10,)),
            dma((80,)),
            dma((3,)),
            dma((4,)),
            dma((4,)),
            dma((2, 4)),
            dma((2,)),
            dma((4, 2)),
            dma((8, 2)),
            dma((2,)),
            dma((2, 4, 2)),
            dma((4,)),
            dma((2, 4, 2)),
            dma((2,)),
            dma((5,)),
        ],
        compiler_params=pltpu.CompilerParams(
            collective_id=0, has_side_effects=True, vmem_limit_bytes=60 * 2**20
        ),
        cost_estimate=pl.CostEstimate(flops=8 * 10**9, bytes_accessed=6 * 2**20, transcendentals=10**6),
    )(queries[0], encoded[0, 0], projection.T, neighbour_shard, neighbour_block)
    return out[None]


def solution(mesh):
    placed = (
        P("dp", "seq", None),
        P("dp", "seq", None, None, None),
        P(None, ("dp", "seq")),
        P("dp", "seq", None),
        P("dp", "seq", None),
    )
    return jax.shard_map(
        body, mesh=mesh, in_specs=placed, out_specs=P("dp", "seq", None), check_vma=False
    )
```

```python
import math

import jax
import jax.numpy as jnp
from jax import lax
from jax.experimental import pallas as pl
from jax.experimental.pallas import tpu as pltpu
from jax.sharding import PartitionSpec as P

MESH = pl.DeviceIdType.MESH
HD = 128
CH = 64
LA = 256
LB = 512
LD = 128
SCALE = 1.0 / math.sqrt(HD)


def dot_nt(a, b):
    return lax.dot_general(a, b, (((1,), (1,)), ((), ())), preferred_element_type=jnp.float32)


def dot_nn(a, b):
    return lax.dot_general(a, b, (((1,), (0,)), ((), ())), preferred_element_type=jnp.float32)


XS = {0: 0, 3: 1, 1: 2, 2: 3}
XR = (0, 3, 1, 2)
ZS = {0: 0, 1: 1, 7: 2, 2: 3, 6: 4, 3: 5, 5: 6, 4: 7}
DO_P1 = DO_P2 = DO_TOK = DO_Q = DO_OUT = DO_MATH = True


def kernel(
    q_ref, enc_hbm, wt_ref, sh_hbm, bl_hbm, out_ref,
    W, KV, enc, pack, recv, tok, q_all, qs, stage, fix, idx_out, idx_in, idx_smem,
    sh_ref, bl_ref,
    lsem, ssem, qsem, osem, s_idx, s_tok, s_sib, s_wx, s_p1y, s_p1z, s_p2z, s_p2y, s_dy, s_dz, s_dx, s_q, s_o,
):
    x = lax.axis_index("dp")
    s = lax.axis_index("seq")
    y = lax.div(s, 16)
    z = lax.rem(lax.div(s, 2), 8)
    k = lax.rem(s, 2)
    yy = lax.div(y, 2)
    cs = lax.rem(y, 2)
    act = cs == k
    pas = jnp.logical_not(act)

    def dev(dx=0, dy=0, dz=0, core=None):
        core = k if core is None else core
        return (
            lax.rem(x + dx + 4, 4),
            lax.rem(y + dy + 4, 4) * 16 + lax.rem(z + dz + 8, 8) * 2 + core,
        )

    def chip_along(step, core):
        return (x, lax.rem(lax.div(s, 2) + step + 32, 32) * 2 + core)

    sib = dev(core=1 - k)
    counter = [0]

    def remote(src, dst, rsem, to):
        n = counter[0]
        counter[0] += 1

        def build():
            return pltpu.make_async_remote_copy(
                src_ref=src, dst_ref=dst, send_sem=ssem.at[n], recv_sem=rsem, device_id=to, device_id_type=MESH
            )

        return build

    def arrived(dst, rsem):
        pltpu.make_async_copy(dst, dst, rsem).wait()

    barrier = pltpu.get_barrier_semaphore()
    partners = [sib]
    for c in (0, 1):
        partners += [dev(dx=d, core=c) for d in (1, 2, 3)]
        partners += [chip_along(1, c), chip_along(-1, c)]
        partners += [dev(dy=d, core=c) for d in (1, 2, 3)]
    partners += [dev(dz=d) for d in (1, -1)]
    for p in partners:
        pl.semaphore_signal(barrier, inc=1, device_id=p, device_id_type=MESH)

    sh_cp = pltpu.make_async_copy(sh_hbm, sh_ref, lsem.at[5])
    bl_cp = pltpu.make_async_copy(bl_hbm, bl_ref, lsem.at[6])
    sh_cp.start()
    bl_cp.start()
    enc_cp = pltpu.make_async_copy(enc_hbm, enc, lsem.at[0])
    enc_cp.start()

    lane = lax.broadcasted_iota(jnp.int32, (8, 128), 1)
    sh_cp.wait()
    bl_cp.wait()
    own_sh = [sh_ref[0, e // 2, e % 2] for e in range(4)]
    own_bl = [bl_ref[0, e // 2, e % 2] for e in range(4)]
    codes = jnp.zeros((8, 128), jnp.int32)
    for e in range(4):
        codes = jnp.where(lane == e, own_sh[e], codes)
        codes = jnp.where(lane == 4 + e, own_bl[e], codes)
    idx_out[...] = codes
    pl.semaphore_wait(barrier, len(partners))

    always, if_act, if_pas = [], [], []

    for d in (1, 2, 3):
        always.append(remote(idx_out, idx_in.at[x], s_idx.at[d], dev(dx=d)))
        always[-1]().start()

    half = pl.ds(pl.multiple_of(k * 32, 32), 32)
    other = pl.ds(pl.multiple_of((1 - k) * 32, 32), 32)
    fa, fb, fd, fab = pl.ds(0, LA), pl.ds(LA, LB), pl.ds(LA + LB, LD), pl.ds(0, LA + LB)
    own = lambda: pltpu.make_async_copy(wt_ref, W.at[0, yy, 0, half], lsem.at[1])
    to_sib_w = remote(wt_ref, W.at[0, yy, 0, half], s_wx.at[0, k], sib)
    if_pas.append(to_sib_w)

    @pl.when(act)
    def _():
        own().start()

    @pl.when(pas)
    def _():
        to_sib_w().start()

    for d in (2, 1, 3):
        always.append(
            remote(wt_ref.at[:, fab], W.at[XS[4 - d], yy, 0, half, fab], s_wx.at[d, k], dev(dx=d, core=cs))
        )
        always[-1]().start()
    for d in (2, 1, 3):
        always.append(remote(wt_ref.at[:, fd], W.at[0, yy, 0, half, fd], s_dy.at[d, k], dev(dy=d, core=cs)))
        always[-1]().start()

    local_rows = pl.ds(pl.multiple_of(k * 128, 128), 128)

    def qcols(g, core):
        return pl.ds(pl.multiple_of(g * 512 + core * 256, 256), 256)

    def gcols(g):
        return pl.ds(pl.multiple_of(g * 256, 256), 256)

    def q_copies(g):
        loc = pltpu.make_async_copy(q_ref.at[:, qcols(g, k)], q_all.at[local_rows, gcols(g)], lsem.at[4])
        to_sib = pltpu.make_async_remote_copy(
            src_ref=q_ref.at[:, qcols(g, 1 - k)], dst_ref=q_all.at[local_rows, gcols(g)],
            send_sem=qsem.at[0], recv_sem=s_q.at[0], device_id=sib, device_id_type=MESH,
        )
        back = [
            pltpu.make_async_remote_copy(
                src_ref=q_ref.at[pl.ds(0, 64), qcols(g, c)], dst_ref=q_all.at[pl.ds(256, 64), gcols(g)],
                send_sem=qsem.at[1 + c], recv_sem=s_q.at[1], device_id=chip_along(-1, c), device_id_type=MESH,
            )
            for c in (0, 1)
        ]
        return loc, to_sib, back

    if DO_Q:
        @pl.loop(0, 8)
        def _(g):
            loc, to_sib, back = q_copies(g)
            loc.start()
            to_sib.start()

            @pl.when(k == 0)
            def _():
                back[0].start()
                back[1].start()

    p1y = [remote(W.at[:, yy, 0, :, fa], W.at[:, yy, 0, :, fa], s_p1y.at[yy], dev(dy=d)) for d in (1, 3, 2)]
    if_act += p1y

    def ends_of(direction, step):
        return (ZS[step - 1], ZS[step]) if direction else (ZS[(9 - step) % 8], ZS[8 - step])

    def zstep(direction, step, part):
        have, there = ends_of(direction, step)
        return remote(
            W.at[:, part, have, :, fa], W.at[:, part, there, :, fa], s_p1z.at[direction, step - 1, part],
            dev(dz=-1 if direction else 1),
        )

    def zwait(direction, step, part):
        arrived(W.at[:, part, ends_of(direction, step)[1], :, fa], s_p1z.at[direction, step - 1, part])

    def dstep(direction, step, part):
        have, there = ends_of(direction, step)
        return remote(
            W.at[0, part, have, :, fd], W.at[0, part, there, :, fd], s_dz.at[direction, step - 1, part],
            dev(dz=-1 if direction else 1),
        )

    def dwait(direction, step, part):
        arrived(W.at[0, part, ends_of(direction, step)[1], :, fd], s_dz.at[direction, step - 1, part])

    PIECES = ((0, 3), (3, 5), (5, 7), (7, 8))
    dx = {}
    for i, (z0, z1) in enumerate(PIECES):
        dx[i] = [
            remote(W.at[0, :, z0:z1, :, fd], W.at[XS[4 - d], :, z0:z1, :, fd], s_dx.at[d, i], dev(dx=d))
            for d in (2, 1, 3)
        ]
        always += dx[i]

    def dxsend(i):
        for t in dx[i]:
            t().start()

    def dxwait(i):
        z0, z1 = PIECES[i]
        for d in (1, 3, 2):
            arrived(W.at[XS[4 - d], :, z0:z1, :, fd], s_dx.at[d, i])

    z_own = [zstep(i, 1, yy) for i in (0, 1)] + [dstep(i, 1, yy) for i in (0, 1)]
    z_far = [zstep(i, 1, 1 - yy) for i in (0, 1)] + [dstep(i, 1, 1 - yy) for i in (0, 1)]
    z_next = {st: [(i, p, zstep(i, st, p), dstep(i, st, p)) for p in (0, 1) for i in (0, 1)] for st in (2, 3)}
    z_next[4] = [(0, 0, zstep(0, 4, 0), dstep(0, 4, 0)), (1, 1, zstep(1, 4, 1), dstep(1, 4, 1))]
    always += z_own + z_far + [t for st in (2, 3, 4) for n in z_next[st] for t in n[2:]]

    def z_forward(st):
        if not DO_P1:
            return
        waited = set()
        for i, p, t, u in z_next[st]:
            zwait(i, st - 1, p)
            dwait(i, st - 1, p)
            waited.add((i, p))
            t().start()
            u().start()
        for i in (0, 1):
            for p in (0, 1):
                if (i, p) not in waited:
                    zwait(i, st - 1, p)
                    dwait(i, st - 1, p)
        dxsend(st - 2)

    def columns_of(direction, step):
        return pl.ds(2 * direction, 2) if step == 4 else pl.ds(0, 4)

    def bstep(direction, step):
        have, there = ends_of(direction, step)
        xs = columns_of(direction, step)
        return remote(
            W.at[xs, yy, have, :, fb], W.at[xs, yy, there, :, fb], s_p2z.at[direction, step - 1],
            dev(dz=-1 if direction else 1),
        )

    def bwait(direction, step):
        arrived(W.at[columns_of(direction, step), yy, ends_of(direction, step)[1], :, fb], s_p2z.at[direction, step - 1])

    b_steps = {st: [bstep(i, st) for i in (0, 1)] for st in (1, 2, 3, 4)}
    for st in (1, 2, 3, 4):
        if_act += b_steps[st]

    def ysend(direction, plane, piece, part):
        ref = W.at[pl.ds(2 * piece, 2), part, ZS[plane], :, fb]
        return remote(ref, ref, s_p2y.at[direction, plane, piece], dev(dy=-1 if direction else 1))

    below, above = lax.div(lax.rem(y + 3, 4), 2), lax.div(lax.rem(y + 1, 4), 2)

    def ywait(direction, plane, piece):
        part = jnp.where(act, 1 - yy, above if direction else below)
        arrived(W.at[pl.ds(2 * piece, 2), part, ZS[plane], :, fb], s_p2y.at[direction, plane, piece])

    y_act = {d: [ysend(0, d, 0, yy), ysend(1, d, 1, yy), ysend(0, d, 1, yy), ysend(1, d, 0, yy)] for d in range(8)}
    y_pas = {d: [ysend(0, d, 0, below), ysend(1, d, 1, above)] for d in range(8)}
    for d in range(8):
        if_act += y_act[d]
        if_pas += y_pas[d]

    def b_forward(st):
        if not DO_P2:
            return
        for i in (0, 1):
            bwait(i, st)
            if st < 4:
                b_steps[st + 1][i]().start() if st < 3 or i == 0 else None
        if st == 3:
            b_steps[4][1]().start()
        for plane in (8 - st, st) if st < 4 else (4,):
            for t in y_act[plane]:
                t().start()

    def y_forward(plane):
        if not DO_P2:
            return
        ywait(0, plane, 0)
        y_pas[plane][0]().start()
        ywait(1, plane, 1)
        y_pas[plane][1]().start()

    def y_rest(plane):
        if not DO_P2:
            return
        ywait(0, plane, 1)
        ywait(1, plane, 0)

    def y_here(plane):
        if not DO_P2:
            return
        ywait(0, plane, 0)
        ywait(1, plane, 1)

    @pl.when(act)
    def _():
        own().wait()
        arrived(W.at[0, yy, 0, other], s_wx.at[0, 1 - k])
        for d in (1, 3, 2):
            for c in (0, 1):
                arrived(W.at[XS[4 - d], yy, 0, pl.ds(c * 32, 32), fab], s_wx.at[d, c])
        if DO_P1:
            for t in p1y:
                t().start()
        if DO_P2:
            for t in b_steps[1] + y_act[0]:
                t().start()
        if DO_P1:
            for t in z_own:
                t().start()

    enc_cp.wait()

    def wanted(sh, bl):
        m = [v == x for v in sh]
        first = jnp.where(m[0], bl[0], jnp.where(m[1], bl[1], jnp.where(m[2], bl[2], bl[3])))
        last = jnp.where(m[3], bl[3], jnp.where(m[2], bl[2], jnp.where(m[1], bl[1], bl[0])))
        return first, last

    to_smem = {}
    for d in (1, 3, 2):
        src = lax.rem(x + d, 4)
        arrived(idx_in.at[src], s_idx.at[4 - d])
        to_smem[d] = pltpu.make_async_copy(idx_in.at[src], idx_smem.at[src], lsem.at[6 + d])
        to_smem[d].start()
    for d in (1, 3, 2):
        src = lax.rem(x + d, 4)
        to_smem[d].wait()
        pair = wanted([idx_smem[src, 0, e] for e in range(4)], [idx_smem[src, 0, 4 + e] for e in range(4)])
        for i in range(2):
            pack[d - 1, i] = enc[pair[i]]
        if DO_TOK:
            always.append(remote(pack.at[d - 1], recv.at[pl.ds(x * 2, 2)], s_tok.at[d], dev(dx=d)))
            always[-1]().start()
    pair = wanted(own_sh, own_bl)
    for i in range(2):
        recv[x * 2 + i] = enc[pair[i]]

    if DO_P1:
        @pl.when(act)
        def _():
            arrived(W.at[:, 1 - yy, 0, :, fa], s_p1y.at[1 - yy])
            for c in (0, 1):
                arrived(W.at[0, 1 - yy, 0, pl.ds(c * 32, 32), fd], s_dy.at[2, c])
            for t in z_far:
                t().start()

        @pl.when(pas)
        def _():
            for part in (0, 1):
                arrived(W.at[:, part, 0, :, fa], s_p1y.at[part])
            for c in (0, 1):
                arrived(W.at[0, below, 0, pl.ds(c * 32, 32), fd], s_dy.at[1, c])
                arrived(W.at[0, above, 0, pl.ds(c * 32, 32), fd], s_dy.at[3, c])
            for t in z_own + z_far:
                t().start()

    @pl.when(act)
    def _():
        b_forward(1)

    @pl.when(pas)
    def _():
        y_forward(0)

    z_forward(2)

    @pl.when(act)
    def _():
        b_forward(2)

    @pl.when(pas)
    def _():
        y_forward(7)
        y_forward(1)

    half_tok = []
    rank = [jnp.int32(0)]
    for e in range(1, 4):
        same = own_sh[e] == own_sh[0]
        for f in range(1, e):
            same = jnp.logical_or(same, own_sh[e] == own_sh[f])
        rank.append(jnp.where(same, 1, 0))

    @pl.when(act)
    def _():
        b_forward(3)

    z_forward(3)

    @pl.when(pas)
    def _():
        y_forward(6)


    if DO_TOK:
        for d in (1, 2, 3):
            arrived(recv.at[pl.ds(lax.rem(x + 4 - d, 4) * 2, 2)], s_tok.at[d])
    for e in range(4):
        tok[k, pl.ds(e * 128, 128)] = recv[own_sh[e] * 2 + rank[e]]
    half_tok.append(remote(tok.at[k], tok.at[k], s_sib.at[0], sib))
    half_tok[-1]().start()

    def project(z0, z1):
        if not DO_MATH:
            return
        rows = 8 * (z1 - z0) * 64
        a = W[:, :, z0:z1].reshape(rows, LA + LB + LD)
        for j in range(4):
            kv = dot_nt(a, tok[j // 2, pl.ds((j % 2) * 256, 256)])
            KV[:, :, z0:z1, :, j * 256 : j * 256 + 256] = kv.astype(jnp.bfloat16).reshape(4, 2, z1 - z0, 64, 256)

    def plane_of(zabs):
        d = lax.rem(zabs - z + 8, 8)
        return jnp.where(d <= 4, jnp.maximum(2 * d - 1, 0), 16 - 2 * d)

    def attend(xs, zh):
        xa = lax.rem(x + XR[xs], 4)
        if not DO_MATH:
            for part in (0, 1):
                stage[xs * 2 + part, :, pl.ds(pl.multiple_of(zh * 128, 128), 128)] = qs[:, 0:128]
            return
        planes = [plane_of(zh * 4 + i) for i in range(4)]
        units = [(part, j) for part in (0, 1) for j in range(4)]
        scores = []
        for part, j in units:
            cols = pl.ds(pl.multiple_of((xa * 2 + part) * 256 + zh * 128, 128), 128)
            at = slice(j * 256, j * 256 + 256)
            keys = jnp.concatenate([KV[xs, part, planes[0], :, at], KV[xs, part, planes[1], :, at]], axis=0)
            scores.append(dot_nn(qs[j * 64 : j * 64 + 64, cols], keys))
        weights = []
        for sc in scores:
            sc = sc * SCALE
            sc = jnp.exp(sc - jnp.max(sc, axis=1, keepdims=True))
            weights.append((sc * (1.0 / jnp.sum(sc, axis=1, keepdims=True))).astype(jnp.bfloat16))
        parts = []
        for (part, j), w in zip(units, weights):
            at = slice(j * 256, j * 256 + 256)
            values = jnp.concatenate([KV[xs, part, planes[2], :, at], KV[xs, part, planes[3], :, at]], axis=0)
            parts.append(dot_nt(w, values))
        for part in (0, 1):
            comb = pltpu.roll(jnp.concatenate(parts[part * 4 : part * 4 + 4], axis=0), 255, 0)
            stage[xs * 2 + part, :, pl.ds(pl.multiple_of(zh * 128, 128), 128)] = comb.astype(jnp.bfloat16)

    def send_out(xs, zh):
        xa = lax.rem(x + XR[xs], 4)
        lanes = pl.ds(pl.multiple_of(zh * 128, 128), 128)
        for part in (0, 1):
            st = stage.at[xs * 2 + part]
            cols = pl.ds(pl.multiple_of((xa * 2 + part) * 512 + k * 256 + zh * 128, 128), 128)

            def to(src, dst, n, target):
                return pltpu.make_async_remote_copy(
                    src_ref=src, dst_ref=dst, send_sem=osem.at[n], recv_sem=s_o.at[n + 1 if n else k],
                    device_id=target, device_id_type=MESH,
                )

            if DO_OUT:
                to(st.at[pl.ds(192, 64), lanes], out_ref.at[pl.ds(0, 64), cols], 0, chip_along(1, 0)).start()

            @pl.when(k == 0)
            def _():
                if DO_OUT:
                    to(st.at[pl.ds(64, 128), lanes], out_ref.at[:, cols], 1, sib).start()
                out_ref[pl.ds(64, 64), cols] = st[pl.ds(0, 64), lanes]
                fix[:, cols] = st[pl.ds(240, 16), lanes]

            @pl.when(k == 1)
            def _():
                if DO_OUT:
                    to(st.at[pl.ds(0, 64), lanes], out_ref.at[pl.ds(64, 64), cols], 2, sib).start()
                    to(st.at[pl.ds(240, 16), lanes], fix.at[:, cols], 3, sib).start()
                out_ref[:, cols] = st[pl.ds(64, 128), lanes]

    near = lax.div(z, 4)

    whole_q = q_all.at[pl.ds(0, 128)]
    if DO_Q:
        pltpu.make_async_copy(q_ref.at[:, pl.ds(0, 2048)], whole_q, lsem.at[4]).wait()
        arrived(whole_q, s_q.at[0])
        arrived(q_all.at[pl.ds(256, 64)], s_q.at[1])

        @pl.loop(0, 8)
        def _(g):
            rows = q_all[pl.ds(48, 272), gcols(g)].astype(jnp.float32)
            qs[:, gcols(g)] = pltpu.roll(rows, 1, 0)[16:].astype(jnp.bfloat16)

    arrived(tok.at[1 - k], s_sib.at[0])

    def here(*planes):
        @pl.when(act)
        def _():
            for plane in planes:
                y_here(plane)

        @pl.when(pas)
        def _():
            for plane in planes:
                y_rest(plane)

    def forward_b(plane):
        @pl.when(pas)
        def _():
            y_forward(plane)

    dxwait(0)
    here(0)
    project(0, 1)

    @pl.when(act)
    def _():
        b_forward(4)

    forward_b(2)
    here(7, 1)
    project(1, 3)
    z_forward(4)
    forward_b(5)
    here(6, 2)
    dxwait(1)
    project(3, 5)
    forward_b(3)
    here(5, 3)
    dxwait(2)
    project(5, 7)
    forward_b(4)
    for xs in range(2):
        attend(xs, near)
        send_out(xs, near)

    if DO_P1:
        for i in (0, 1):
            zwait(i, 4, i)
            dwait(i, 4, i)
        dxsend(3)

    for xs in range(2, 4):
        attend(xs, near)
        send_out(xs, near)

    @pl.when(act)
    def _():
        y_here(4)

    @pl.when(pas)
    def _():
        y_rest(4)

    dxwait(3)
    project(7, 8)

    skip = set()
    for t in always + half_tok:
        if t not in skip:
            t().wait_send()

    @pl.when(act)
    def _():
        for t in if_act:
            if t not in skip:
                t().wait_send()

    @pl.when(pas)
    def _():
        for t in if_pas:
            if t not in skip:
                t().wait_send()

    if DO_Q:
        arrived(whole_q, qsem.at[0])

        @pl.when(k == 0)
        def _():
            arrived(q_all.at[pl.ds(0, 64)], qsem.at[1])
            arrived(q_all.at[pl.ds(0, 64)], qsem.at[2])

    for xs in range(4):
        attend(xs, 1 - near)
        send_out(xs, 1 - near)

    sixty_four = q_all.at[pl.ds(0, 64)]
    sixteen = q_all.at[pl.ds(0, 16)]
    if DO_OUT:
        arrived(sixty_four, osem.at[0])

        @pl.when(k == 0)
        def _():
            arrived(whole_q, osem.at[1])
            arrived(sixty_four, s_o.at[0])
            arrived(sixty_four, s_o.at[1])
            arrived(sixty_four, s_o.at[3])
            arrived(sixteen, s_o.at[4])
            first = s == 0

            @pl.when(first)
            def _():
                out_ref[pl.ds(0, 48)] = jnp.zeros((48, 4096), jnp.bfloat16)

            @pl.loop(0, 8)
            def _(g):
                cols = pl.ds(pl.multiple_of(g * 512, 512), 512)
                row = lax.broadcasted_iota(jnp.int32, (16, 512), 0)
                came = out_ref[pl.ds(48, 16), cols].astype(jnp.float32)
                came = jnp.where(first, 0.0, came)
                own = fix[:, cols].astype(jnp.float32)
                out_ref[pl.ds(48, 16), cols] = jnp.where(row == 15, own, came).astype(jnp.bfloat16)

        @pl.when(k == 1)
        def _():
            arrived(sixty_four, osem.at[2])
            arrived(sixteen, osem.at[3])
            arrived(whole_q, s_o.at[2])


def body(queries, encoded, projection, neighbour_shard, neighbour_block):
    bf = jnp.bfloat16
    dma = pltpu.SemaphoreType.DMA
    hbm = pl.BlockSpec(memory_space=pl.ANY)
    out = pl.pallas_call(
        kernel,
        name="spans",
        out_shape=jax.ShapeDtypeStruct((128, 4096), bf),
        in_specs=[hbm] * 5,
        out_specs=pl.BlockSpec(memory_space=pltpu.VMEM),
        scratch_shapes=[
            pltpu.VMEM((4, 2, 8, 64, LA + LB + LD), bf),
            pltpu.VMEM((4, 2, 8, 64, 1024), bf),
            pltpu.VMEM((12, 128, 896), bf),
            pltpu.VMEM((3, 2, 128, 896), bf),
            pltpu.VMEM((8, 128, 896), bf),
            pltpu.VMEM((2, 512, 896), bf),
            pltpu.VMEM((320, 2048), bf),
            pltpu.VMEM((256, 2048), bf),
            pltpu.VMEM((8, 256, 256), bf),
            pltpu.VMEM((16, 4096), bf),
            pltpu.VMEM((8, 128), jnp.int32),
            pltpu.VMEM((4, 8, 128), jnp.int32),
            pltpu.SMEM((4, 8, 128), jnp.int32),
            pltpu.SMEM((1, 2, 2), jnp.int32),
            pltpu.SMEM((1, 2, 2), jnp.int32),
            dma((10,)),
            dma((130,)),
            dma((3,)),
            dma((4,)),
            dma((4,)),
            dma((4,)),
            dma((1,)),
            dma((4, 2)),
            dma((2,)),
            dma((2, 4, 2)),
            dma((2, 4)),
            dma((2, 8, 2)),
            dma((4, 2)),
            dma((2, 4, 2)),
            dma((4, 4)),
            dma((2,)),
            dma((5,)),
        ],
        compiler_params=pltpu.CompilerParams(
            collective_id=0, has_side_effects=True, vmem_limit_bytes=60 * 2**20
        ),
        cost_estimate=pl.CostEstimate(flops=8 * 10**9, bytes_accessed=6 * 2**20, transcendentals=10**6),
    )(queries[0], encoded[0, 0], projection.T, neighbour_shard, neighbour_block)
    return out[None]


def solution(mesh):
    placed = (
        P("dp", "seq", None),
        P("dp", "seq", None, None, None),
        P(None, ("dp", "seq")),
        P("dp", "seq", None),
        P("dp", "seq", None),
    )
    return jax.shard_map(
        body, mesh=mesh, in_specs=placed, out_specs=P("dp", "seq", None), check_vma=False
    )
```

```python
import math

import jax
import jax.numpy as jnp
from jax import lax
from jax.experimental import pallas as pl
from jax.experimental.pallas import tpu as pltpu
from jax.sharding import PartitionSpec as P

MESH = pl.DeviceIdType.MESH
HD = 128
CH = 64
LA = 256
LB = 512
LD = 128
SCALE = 1.0 / math.sqrt(HD)


def dot_nt(a, b):
    return lax.dot_general(a, b, (((1,), (1,)), ((), ())), preferred_element_type=jnp.float32)


def dot_nn(a, b):
    return lax.dot_general(a, b, (((1,), (0,)), ((), ())), preferred_element_type=jnp.float32)


XS = {0: 0, 3: 1, 1: 2, 2: 3}
XR = (0, 3, 1, 2)
ZS = {0: 0, 1: 1, 7: 2, 2: 3, 6: 4, 3: 5, 5: 6, 4: 7}


def kernel(
    q_ref, enc_hbm, wt_ref, sh_hbm, bl_hbm, out_ref,
    W, KV, enc, pack, recv, tok, q_all, qs, stage, fix, idx_out, idx_in, idx_smem,
    sh_ref, bl_ref,
    lsem, ssem, qsem, osem, s_idx, s_tok, s_sib, s_wx, s_p1y, s_p1z, s_p2z, s_p2y, s_dy, s_dz, s_dx, s_q, s_o,
):
    x = lax.axis_index("dp")
    s = lax.axis_index("seq")
    y = lax.div(s, 16)
    z = lax.rem(lax.div(s, 2), 8)
    k = lax.rem(s, 2)
    yy = lax.div(y, 2)
    cs = lax.rem(y, 2)
    act = cs == k
    pas = jnp.logical_not(act)

    def dev(dx=0, dy=0, dz=0, core=None):
        core = k if core is None else core
        return (
            lax.rem(x + dx + 4, 4),
            lax.rem(y + dy + 4, 4) * 16 + lax.rem(z + dz + 8, 8) * 2 + core,
        )

    def chip_along(step, core):
        return (x, lax.rem(lax.div(s, 2) + step + 32, 32) * 2 + core)

    sib = dev(core=1 - k)
    counter = [0]

    def remote(src, dst, rsem, to):
        n = counter[0]
        counter[0] += 1

        def build():
            return pltpu.make_async_remote_copy(
                src_ref=src, dst_ref=dst, send_sem=ssem.at[n], recv_sem=rsem, device_id=to, device_id_type=MESH
            )

        return build

    def arrived(dst, rsem):
        pltpu.make_async_copy(dst, dst, rsem).wait()

    barrier = pltpu.get_barrier_semaphore()
    partners = [sib]
    for c in (0, 1):
        partners += [dev(dx=d, core=c) for d in (1, 2, 3)]
        partners += [chip_along(1, c), chip_along(-1, c)]
        partners += [dev(dy=d, core=c) for d in (1, 2, 3)]
    partners += [dev(dz=d) for d in (1, -1)]
    for p in partners:
        pl.semaphore_signal(barrier, inc=1, device_id=p, device_id_type=MESH)

    sh_cp = pltpu.make_async_copy(sh_hbm, sh_ref, lsem.at[5])
    bl_cp = pltpu.make_async_copy(bl_hbm, bl_ref, lsem.at[6])
    sh_cp.start()
    bl_cp.start()
    enc_cp = pltpu.make_async_copy(enc_hbm, enc, lsem.at[0])
    enc_cp.start()

    lane = lax.broadcasted_iota(jnp.int32, (8, 128), 1)
    sh_cp.wait()
    bl_cp.wait()
    own_sh = [sh_ref[0, e // 2, e % 2] for e in range(4)]
    own_bl = [bl_ref[0, e // 2, e % 2] for e in range(4)]
    codes = jnp.zeros((8, 128), jnp.int32)
    for e in range(4):
        codes = jnp.where(lane == e, own_sh[e], codes)
        codes = jnp.where(lane == 4 + e, own_bl[e], codes)
    idx_out[...] = codes
    pl.semaphore_wait(barrier, len(partners))

    always, if_act, if_pas = [], [], []

    for d in (1, 2, 3):
        always.append(remote(idx_out, idx_in.at[x], s_idx.at[d], dev(dx=d)))
        always[-1]().start()

    half = pl.ds(pl.multiple_of(k * 32, 32), 32)
    other = pl.ds(pl.multiple_of((1 - k) * 32, 32), 32)
    fa, fb, fd, fab = pl.ds(0, LA), pl.ds(LA, LB), pl.ds(LA + LB, LD), pl.ds(0, LA + LB)
    own = lambda: pltpu.make_async_copy(wt_ref, W.at[0, yy, 0, half], lsem.at[1])
    to_sib_w = remote(wt_ref, W.at[0, yy, 0, half], s_wx.at[0, k], sib)
    if_pas.append(to_sib_w)

    @pl.when(act)
    def _():
        own().start()

    @pl.when(pas)
    def _():
        to_sib_w().start()

    for d in (2, 1, 3):
        always.append(
            remote(wt_ref.at[:, fab], W.at[XS[4 - d], yy, 0, half, fab], s_wx.at[d, k], dev(dx=d, core=cs))
        )
        always[-1]().start()
    for d in (2, 1, 3):
        always.append(remote(wt_ref.at[:, fd], W.at[0, yy, 0, half, fd], s_dy.at[d, k], dev(dy=d, core=cs)))
        always[-1]().start()

    local_rows = pl.ds(pl.multiple_of(k * 128, 128), 128)

    def qcols(g, core):
        return pl.ds(pl.multiple_of(g * 512 + core * 256, 256), 256)

    def gcols(g):
        return pl.ds(pl.multiple_of(g * 256, 256), 256)

    def q_copies(g):
        loc = pltpu.make_async_copy(q_ref.at[:, qcols(g, k)], q_all.at[local_rows, gcols(g)], lsem.at[4])
        to_sib = pltpu.make_async_remote_copy(
            src_ref=q_ref.at[:, qcols(g, 1 - k)], dst_ref=q_all.at[local_rows, gcols(g)],
            send_sem=qsem.at[0], recv_sem=s_q.at[0], device_id=sib, device_id_type=MESH,
        )
        back = [
            pltpu.make_async_remote_copy(
                src_ref=q_ref.at[pl.ds(0, 64), qcols(g, c)], dst_ref=q_all.at[pl.ds(256, 64), gcols(g)],
                send_sem=qsem.at[1 + c], recv_sem=s_q.at[1], device_id=chip_along(-1, c), device_id_type=MESH,
            )
            for c in (0, 1)
        ]
        return loc, to_sib, back

    @pl.loop(0, 8)
    def _(g):
        loc, to_sib, back = q_copies(g)
        loc.start()
        to_sib.start()

        @pl.when(k == 0)
        def _():
            back[0].start()
            back[1].start()

    p1y = [remote(W.at[:, yy, 0, :, fa], W.at[:, yy, 0, :, fa], s_p1y.at[yy], dev(dy=d)) for d in (1, 3, 2)]
    if_act += p1y

    def ends_of(direction, step):
        return (ZS[step - 1], ZS[step]) if direction else (ZS[(9 - step) % 8], ZS[8 - step])

    def zstep(direction, step, part):
        have, there = ends_of(direction, step)
        return remote(
            W.at[:, part, have, :, fa], W.at[:, part, there, :, fa], s_p1z.at[direction, step - 1, part],
            dev(dz=-1 if direction else 1),
        )

    def zwait(direction, step, part):
        arrived(W.at[:, part, ends_of(direction, step)[1], :, fa], s_p1z.at[direction, step - 1, part])

    def dstep(direction, step, part):
        have, there = ends_of(direction, step)
        return remote(
            W.at[0, part, have, :, fd], W.at[0, part, there, :, fd], s_dz.at[direction, step - 1, part],
            dev(dz=-1 if direction else 1),
        )

    def dwait(direction, step, part):
        arrived(W.at[0, part, ends_of(direction, step)[1], :, fd], s_dz.at[direction, step - 1, part])

    PIECES = ((0, 3), (3, 5), (5, 7), (7, 8))
    dx = {}
    for i, (z0, z1) in enumerate(PIECES):
        dx[i] = [
            remote(W.at[0, :, z0:z1, :, fd], W.at[XS[4 - d], :, z0:z1, :, fd], s_dx.at[d, i], dev(dx=d))
            for d in (2, 1, 3)
        ]
        always += dx[i]

    def dxsend(i):
        for t in dx[i]:
            t().start()

    def dxwait(i):
        z0, z1 = PIECES[i]
        for d in (1, 3, 2):
            arrived(W.at[XS[4 - d], :, z0:z1, :, fd], s_dx.at[d, i])

    z_own = [zstep(i, 1, yy) for i in (0, 1)] + [dstep(i, 1, yy) for i in (0, 1)]
    z_far = [zstep(i, 1, 1 - yy) for i in (0, 1)] + [dstep(i, 1, 1 - yy) for i in (0, 1)]
    z_next = {st: [(i, p, zstep(i, st, p), dstep(i, st, p)) for p in (0, 1) for i in (0, 1)] for st in (2, 3)}
    z_next[4] = [(0, 0, zstep(0, 4, 0), dstep(0, 4, 0)), (1, 1, zstep(1, 4, 1), dstep(1, 4, 1))]
    always += z_own + z_far + [t for st in (2, 3, 4) for n in z_next[st] for t in n[2:]]

    def z_forward(st):
        waited = set()
        for i, p, t, u in z_next[st]:
            zwait(i, st - 1, p)
            dwait(i, st - 1, p)
            waited.add((i, p))
            t().start()
            u().start()
        for i in (0, 1):
            for p in (0, 1):
                if (i, p) not in waited:
                    zwait(i, st - 1, p)
                    dwait(i, st - 1, p)
        dxsend(st - 2)

    def columns_of(direction, step):
        return pl.ds(2 * direction, 2) if step == 4 else pl.ds(0, 4)

    def bstep(direction, step):
        have, there = ends_of(direction, step)
        xs = columns_of(direction, step)
        return remote(
            W.at[xs, yy, have, :, fb], W.at[xs, yy, there, :, fb], s_p2z.at[direction, step - 1],
            dev(dz=-1 if direction else 1),
        )

    def bwait(direction, step):
        arrived(W.at[columns_of(direction, step), yy, ends_of(direction, step)[1], :, fb], s_p2z.at[direction, step - 1])

    b_steps = {st: [bstep(i, st) for i in (0, 1)] for st in (1, 2, 3, 4)}
    for st in (1, 2, 3, 4):
        if_act += b_steps[st]

    def ysend(direction, plane, piece, part):
        ref = W.at[pl.ds(2 * piece, 2), part, ZS[plane], :, fb]
        return remote(ref, ref, s_p2y.at[direction, plane, piece], dev(dy=-1 if direction else 1))

    below, above = lax.div(lax.rem(y + 3, 4), 2), lax.div(lax.rem(y + 1, 4), 2)

    def ywait(direction, plane, piece):
        part = jnp.where(act, 1 - yy, above if direction else below)
        arrived(W.at[pl.ds(2 * piece, 2), part, ZS[plane], :, fb], s_p2y.at[direction, plane, piece])

    y_act = {d: [ysend(0, d, 0, yy), ysend(1, d, 1, yy), ysend(0, d, 1, yy), ysend(1, d, 0, yy)] for d in range(8)}
    y_pas = {d: [ysend(0, d, 0, below), ysend(1, d, 1, above)] for d in range(8)}
    for d in range(8):
        if_act += y_act[d]
        if_pas += y_pas[d]

    def b_forward(st):
        for i in (0, 1):
            bwait(i, st)
            if st < 4:
                b_steps[st + 1][i]().start() if st < 3 or i == 0 else None
        if st == 3:
            b_steps[4][1]().start()
        for plane in (8 - st, st) if st < 4 else (4,):
            for t in y_act[plane]:
                t().start()

    def y_forward(plane):
        ywait(0, plane, 0)
        y_pas[plane][0]().start()
        ywait(1, plane, 1)
        y_pas[plane][1]().start()

    def y_rest(plane):
        ywait(0, plane, 1)
        ywait(1, plane, 0)

    def y_here(plane):
        ywait(0, plane, 0)
        ywait(1, plane, 1)

    @pl.when(act)
    def _():
        own().wait()
        arrived(W.at[0, yy, 0, other], s_wx.at[0, 1 - k])
        for d in (1, 3, 2):
            for c in (0, 1):
                arrived(W.at[XS[4 - d], yy, 0, pl.ds(c * 32, 32), fab], s_wx.at[d, c])
        for t in p1y:
            t().start()
        for t in b_steps[1] + y_act[0]:
            t().start()
        for t in z_own:
            t().start()

    enc_cp.wait()

    def wanted(sh, bl):
        m = [v == x for v in sh]
        first = jnp.where(m[0], bl[0], jnp.where(m[1], bl[1], jnp.where(m[2], bl[2], bl[3])))
        last = jnp.where(m[3], bl[3], jnp.where(m[2], bl[2], jnp.where(m[1], bl[1], bl[0])))
        return first, last

    to_smem = {}
    for d in (1, 3, 2):
        src = lax.rem(x + d, 4)
        arrived(idx_in.at[src], s_idx.at[4 - d])
        to_smem[d] = pltpu.make_async_copy(idx_in.at[src], idx_smem.at[src], lsem.at[6 + d])
        to_smem[d].start()
    for d in (2, 1, 3):
        src = lax.rem(x + d, 4)
        to_smem[d].wait()
        pair = wanted([idx_smem[src, 0, e] for e in range(4)], [idx_smem[src, 0, 4 + e] for e in range(4)])
        for i in range(2):
            pack[d - 1, i] = enc[pair[i]]
        always.append(remote(pack.at[d - 1], recv.at[pl.ds(x * 2, 2)], s_tok.at[d], dev(dx=d)))
        always[-1]().start()
    pair = wanted(own_sh, own_bl)
    for i in range(2):
        recv[x * 2 + i] = enc[pair[i]]

    @pl.when(act)
    def _():
        arrived(W.at[:, 1 - yy, 0, :, fa], s_p1y.at[1 - yy])
        for c in (0, 1):
            arrived(W.at[0, 1 - yy, 0, pl.ds(c * 32, 32), fd], s_dy.at[2, c])
        for t in z_far:
            t().start()

    @pl.when(pas)
    def _():
        for part in (0, 1):
            arrived(W.at[:, part, 0, :, fa], s_p1y.at[part])
        for c in (0, 1):
            arrived(W.at[0, below, 0, pl.ds(c * 32, 32), fd], s_dy.at[1, c])
            arrived(W.at[0, above, 0, pl.ds(c * 32, 32), fd], s_dy.at[3, c])
        for t in z_own + z_far:
            t().start()

    @pl.when(act)
    def _():
        b_forward(1)

    @pl.when(pas)
    def _():
        y_forward(0)

    z_forward(2)

    @pl.when(act)
    def _():
        b_forward(2)

    @pl.when(pas)
    def _():
        y_forward(7)
        y_forward(1)

    half_tok = []
    rank = [jnp.int32(0)]
    for e in range(1, 4):
        same = own_sh[e] == own_sh[0]
        for f in range(1, e):
            same = jnp.logical_or(same, own_sh[e] == own_sh[f])
        rank.append(jnp.where(same, 1, 0))

    @pl.when(act)
    def _():
        b_forward(3)

    z_forward(3)

    @pl.when(pas)
    def _():
        y_forward(6)


    for d in (1, 2, 3):
        arrived(recv.at[pl.ds(lax.rem(x + 4 - d, 4) * 2, 2)], s_tok.at[d])
    for e in range(4):
        tok[k, pl.ds(e * 128, 128)] = recv[own_sh[e] * 2 + rank[e]]
    half_tok.append(remote(tok.at[k], tok.at[k], s_sib.at[0], sib))
    half_tok[-1]().start()

    def project(z0, z1):
        rows = 8 * (z1 - z0) * 64
        a = W[:, :, z0:z1].reshape(rows, LA + LB + LD)
        for j in range(4):
            kv = dot_nt(a, tok[j // 2, pl.ds((j % 2) * 256, 256)])
            KV[:, :, z0:z1, :, j * 256 : j * 256 + 256] = kv.astype(jnp.bfloat16).reshape(4, 2, z1 - z0, 64, 256)

    def plane_of(zabs):
        d = lax.rem(zabs - z + 8, 8)
        return jnp.where(d <= 4, jnp.maximum(2 * d - 1, 0), 16 - 2 * d)

    def attend(columns, zh):
        lanes = pl.ds(pl.multiple_of(zh * 128, 128), 128)
        planes = [plane_of(zh * 4 + i) for i in range(4)]
        units = [(xs, part, j) for xs in columns for part in (0, 1) for j in range(4)]
        scores = []
        for xs, part, j in units:
            xa = lax.rem(x + XR[xs], 4)
            cols = pl.ds(pl.multiple_of((xa * 2 + part) * 256 + zh * 128, 128), 128)
            at = slice(j * 256, j * 256 + 256)
            keys = jnp.concatenate([KV[xs, part, planes[0], :, at], KV[xs, part, planes[1], :, at]], axis=0)
            scores.append(dot_nn(qs[j * 64 : j * 64 + 64, cols], keys))
        weights = []
        for sc in scores:
            sc = sc * SCALE
            sc = jnp.exp(sc - jnp.max(sc, axis=1, keepdims=True))
            weights.append((sc * (1.0 / jnp.sum(sc, axis=1, keepdims=True))).astype(jnp.bfloat16))
        parts = []
        for (xs, part, j), w in zip(units, weights):
            at = slice(j * 256, j * 256 + 256)
            values = jnp.concatenate([KV[xs, part, planes[2], :, at], KV[xs, part, planes[3], :, at]], axis=0)
            parts.append(dot_nt(w, values))
        for n, xs in enumerate(columns):
            for part in (0, 1):
                first = (n * 2 + part) * 4
                comb = pltpu.roll(jnp.concatenate(parts[first : first + 4], axis=0), 255, 0)
                stage[xs * 2 + part, :, lanes] = comb.astype(jnp.bfloat16)
        for xs in columns:
            send_out(xs, zh)

    def send_out(xs, zh):
        xa = lax.rem(x + XR[xs], 4)
        lanes = pl.ds(pl.multiple_of(zh * 128, 128), 128)
        for part in (0, 1):
            st = stage.at[xs * 2 + part]
            cols = pl.ds(pl.multiple_of((xa * 2 + part) * 512 + k * 256 + zh * 128, 128), 128)

            def to(src, dst, n, target):
                return pltpu.make_async_remote_copy(
                    src_ref=src, dst_ref=dst, send_sem=osem.at[n], recv_sem=s_o.at[n + 1 if n else k],
                    device_id=target, device_id_type=MESH,
                )

            to(st.at[pl.ds(192, 64), lanes], out_ref.at[pl.ds(0, 64), cols], 0, chip_along(1, 0)).start()

            @pl.when(k == 0)
            def _():
                to(st.at[pl.ds(64, 128), lanes], out_ref.at[:, cols], 1, sib).start()
                out_ref[pl.ds(64, 64), cols] = st[pl.ds(0, 64), lanes]
                fix[:, cols] = st[pl.ds(240, 16), lanes]

            @pl.when(k == 1)
            def _():
                to(st.at[pl.ds(0, 64), lanes], out_ref.at[pl.ds(64, 64), cols], 2, sib).start()
                to(st.at[pl.ds(240, 16), lanes], fix.at[:, cols], 3, sib).start()
                out_ref[:, cols] = st[pl.ds(64, 128), lanes]

    near = lax.div(z, 4)

    whole_q = q_all.at[pl.ds(0, 128)]
    pltpu.make_async_copy(q_ref.at[:, pl.ds(0, 2048)], whole_q, lsem.at[4]).wait()
    arrived(whole_q, s_q.at[0])
    arrived(q_all.at[pl.ds(256, 64)], s_q.at[1])

    @pl.loop(0, 8)
    def _(g):
        rows = q_all[pl.ds(48, 272), gcols(g)].astype(jnp.float32)
        qs[:, gcols(g)] = pltpu.roll(rows, 1, 0)[16:].astype(jnp.bfloat16)

    arrived(tok.at[1 - k], s_sib.at[0])

    def here(*planes):
        @pl.when(act)
        def _():
            for plane in planes:
                y_here(plane)

        @pl.when(pas)
        def _():
            for plane in planes:
                y_rest(plane)

    def forward_b(plane):
        @pl.when(pas)
        def _():
            y_forward(plane)

    dxwait(0)
    here(0)
    project(0, 1)

    @pl.when(act)
    def _():
        b_forward(4)

    forward_b(2)
    here(7, 1)
    project(1, 3)
    z_forward(4)
    forward_b(5)
    here(6, 2)
    dxwait(1)
    project(3, 5)
    forward_b(3)
    here(5, 3)
    dxwait(2)
    project(5, 7)
    forward_b(4)
    attend((0, 1), near)

    for i in (0, 1):
        zwait(i, 4, i)
        dwait(i, 4, i)
    dxsend(3)

    attend((2, 3), near)

    @pl.when(act)
    def _():
        y_here(4)

    @pl.when(pas)
    def _():
        y_rest(4)

    dxwait(3)
    project(7, 8)

    for t in always + half_tok:
        t().wait_send()

    @pl.when(act)
    def _():
        for t in if_act:
            t().wait_send()

    @pl.when(pas)
    def _():
        for t in if_pas:
            t().wait_send()

    arrived(whole_q, qsem.at[0])

    @pl.when(k == 0)
    def _():
        arrived(q_all.at[pl.ds(0, 64)], qsem.at[1])
        arrived(q_all.at[pl.ds(0, 64)], qsem.at[2])

    attend((0, 1, 2, 3), 1 - near)

    sixty_four = q_all.at[pl.ds(0, 64)]
    sixteen = q_all.at[pl.ds(0, 16)]
    arrived(sixty_four, osem.at[0])

    @pl.when(k == 0)
    def _():
        arrived(whole_q, osem.at[1])
        arrived(sixty_four, s_o.at[0])
        arrived(sixty_four, s_o.at[1])
        arrived(sixty_four, s_o.at[3])
        arrived(sixteen, s_o.at[4])
        first = s == 0

        @pl.when(first)
        def _():
            out_ref[pl.ds(0, 48)] = jnp.zeros((48, 4096), jnp.bfloat16)

        @pl.loop(0, 8)
        def _(g):
            cols = pl.ds(pl.multiple_of(g * 512, 512), 512)
            row = lax.broadcasted_iota(jnp.int32, (16, 512), 0)
            came = out_ref[pl.ds(48, 16), cols].astype(jnp.float32)
            came = jnp.where(first, 0.0, came)
            own = fix[:, cols].astype(jnp.float32)
            out_ref[pl.ds(48, 16), cols] = jnp.where(row == 15, own, came).astype(jnp.bfloat16)

    @pl.when(k == 1)
    def _():
        arrived(sixty_four, osem.at[2])
        arrived(sixteen, osem.at[3])
        arrived(whole_q, s_o.at[2])


def body(queries, encoded, projection, neighbour_shard, neighbour_block):
    bf = jnp.bfloat16
    dma = pltpu.SemaphoreType.DMA
    hbm = pl.BlockSpec(memory_space=pl.ANY)
    out = pl.pallas_call(
        kernel,
        name="spans",
        out_shape=jax.ShapeDtypeStruct((128, 4096), bf),
        in_specs=[hbm] * 5,
        out_specs=pl.BlockSpec(memory_space=pltpu.VMEM),
        scratch_shapes=[
            pltpu.VMEM((4, 2, 8, 64, LA + LB + LD), bf),
            pltpu.VMEM((4, 2, 8, 64, 1024), bf),
            pltpu.VMEM((12, 128, 896), bf),
            pltpu.VMEM((3, 2, 128, 896), bf),
            pltpu.VMEM((8, 128, 896), bf),
            pltpu.VMEM((2, 512, 896), bf),
            pltpu.VMEM((320, 2048), bf),
            pltpu.VMEM((256, 2048), bf),
            pltpu.VMEM((8, 256, 256), bf),
            pltpu.VMEM((16, 4096), bf),
            pltpu.VMEM((8, 128), jnp.int32),
            pltpu.VMEM((4, 8, 128), jnp.int32),
            pltpu.SMEM((4, 8, 128), jnp.int32),
            pltpu.SMEM((1, 2, 2), jnp.int32),
            pltpu.SMEM((1, 2, 2), jnp.int32),
            dma((10,)),
            dma((130,)),
            dma((3,)),
            dma((4,)),
            dma((4,)),
            dma((4,)),
            dma((1,)),
            dma((4, 2)),
            dma((2,)),
            dma((2, 4, 2)),
            dma((2, 4)),
            dma((2, 8, 2)),
            dma((4, 2)),
            dma((2, 4, 2)),
            dma((4, 4)),
            dma((2,)),
            dma((5,)),
        ],
        compiler_params=pltpu.CompilerParams(
            collective_id=0, has_side_effects=True, vmem_limit_bytes=60 * 2**20
        ),
        cost_estimate=pl.CostEstimate(flops=8 * 10**9, bytes_accessed=6 * 2**20, transcendentals=10**6),
    )(queries[0], encoded[0, 0], projection.T, neighbour_shard, neighbour_block)
    return out[None]


def solution(mesh):
    placed = (
        P("dp", "seq", None),
        P("dp", "seq", None, None, None),
        P(None, ("dp", "seq")),
        P("dp", "seq", None),
        P("dp", "seq", None),
    )
    return jax.shard_map(
        body, mesh=mesh, in_specs=placed, out_specs=P("dp", "seq", None), check_vma=False
    )
```
